32 devices in a mesh: tile: 8 (over z, y), layer: 4 (over x, core).
Axes of the slice: x: 2, y: 2, z: 4, core: 2. Of those that a mesh axis runs over, the one named last changes fastest.
Arguments:
- velocity_guess: float32 [2, 64, 3072], P(None, 'tile'), may hold values from -6 to 6
- hardness: float32 [16, 64, 3072], P('layer', 'tile'), may hold values from 0.7 to 1.5
- thickness: float32 [64, 3072], P('tile'), may hold values from 0.5 to 2
- friction: float32 [64, 3072], P('tile'), may hold values from 0.5 to 5
- grounded: int32 [64, 3072], P('tile'), may hold values 0 or 1
- ice_mask: int32 [64, 3072], P('tile'), may hold values 0 or 1
- driving: float32 [2, 64, 3072], P(None, 'tile'), may hold values from -8 to 8
- obs_cell: int32 [8, 4, 8, 512], P('tile', 'layer'), may hold values from 0 to 24575
- obs_east: float32 [8, 4, 8, 512], P('tile', 'layer'), may hold values from -6 to 6
- obs_north: float32 [8, 4, 8, 512], P('tile', 'layer'), may hold values from -6 to 6
- obs_weight: float32 [8, 4, 8, 512], P('tile', 'layer'), may hold values from 0.1 to 1
- obs_count: int32 [8, 4, 8], P('tile', 'layer'), may hold values from 64 to 512, as said below
Outputs:
- velocity: float32 [2, 64, 3072], P(None, 'tile')
- friction_gradient: float32 [64, 3072], P('tile')
The draws below stay inside these ranges and needn't reach their ends.
Inputs may be any that keep to these rules, and one draw needn't show every extreme that they name: `obs_count`: counts lie between 64 and 512; in every draw one destination strip receives full blocks from every device. `obs_cell`: cells are numbered row by row within the destination strip.
All inputs are finite; a program needn't handle non-finite values. No bound on the sum of `grounded` or of `ice_mask` on one device may be relied on, other than what follows from the above.
Results may differ from the reference program's by a relative error of at most 0.00013.
Values sent between devices are 32-bit elements; how exact they have to be, the bound alone decides.
A program may use at most 64 MiB of HBM per device.

```python
import math
import jax
import jax.numpy as jnp
from jax import lax

CX = 8
NY = 3072
SWEEPS = 40
BLOCK = 512
NX = 64
LAYERS = 16
N_TILE = 8
N_LAYER = 4


def draw_obs_count(key, part):
    first_key, second_key = jax.random.split(jax.random.fold_in(key, 17))
    busiest = jax.random.randint(first_key, (), 0, N_TILE)
    counts = jax.random.randint(second_key, (N_TILE, N_LAYER, N_TILE), BLOCK // 8, BLOCK // 2 + 1)
    target = jnp.arange(N_TILE, dtype=jnp.int32)[None, None, :]
    return jnp.where(target == busiest, BLOCK, counts).astype(jnp.int32)


def plant(entries, own_key, least, top_value):
    longest = entries.shape.index(max(entries.shape))
    spots = []
    for shift in (0, 1):
        where = [jax.random.randint(jax.random.fold_in(own_key, axis), (), 0, length) for axis, length in enumerate(entries.shape)]
        where[longest] = (where[longest] + shift) % entries.shape[longest]
        spots.append(tuple(where))
    return entries.at[spots[0]].set(least).at[spots[1]].set(top_value)


def levels(rng, shape, cuts, low, top_value):
    def one(axis_at, parts):
        draws = jax.random.uniform(jax.random.fold_in(jax.random.fold_in(rng, 6), axis_at), (parts,), jnp.float32, low / len(cuts), top_value / len(cuts))
        return jnp.repeat(jnp.exp(draws), shape[axis_at] // parts).reshape((-1,) + (1,) * (len(shape) - axis_at - 1))

    factor_of = one(*cuts[0])
    for cut in cuts[1:]:
        factor_of = factor_of * one(*cut)
    return factor_of


def bell_draw(stream_key, dims, deviation, bound, cuts=(), held_as=jnp.bfloat16):
    values = deviation * jax.random.normal(stream_key, dims, jnp.float32)
    if cuts:
        values = values * levels(stream_key, dims, cuts, -0.22, 0.18)
    return jnp.clip(values, -bound, bound).astype(held_as)


def setup_inputs(seed: int = 0) -> dict:
    key_of = jax.random.split(jax.random.key(seed), 13)
    return {
        "velocity_guess": bell_draw(key_of[0], (2, NX, NY), 1.0, 6.0, ((1, 8),), jnp.float32),
        "hardness": jnp.clip(jnp.exp(math.log(1.5) - 0.7621401 * jax.random.uniform(key_of[1], (LAYERS, NX, NY), jnp.float32) ** levels(key_of[1], (LAYERS, NX, NY), ((0, 4), (1, 8)), -0.2, 0.2)), 0.7, 1.5),
        "thickness": jnp.clip(0.5 + 1.5 * jax.random.uniform(key_of[2], (NX, NY), jnp.float32) ** levels(key_of[2], (NX, NY), ((0, 8),), -0.2, 0.2), 0.5, 2.0),
        "friction": jnp.clip(jnp.exp(math.log(5.0) - 2.3025851 * jax.random.uniform(key_of[3], (NX, NY), jnp.float32) ** levels(key_of[3], (NX, NY), ((0, 8),), -0.2, 0.2)), 0.5, 5.0),
        "grounded": plant((jax.random.randint(key_of[4], (NX, NY), 0, 10) < 7).astype(jnp.int32), jax.random.fold_in(key_of[4], 1), 0, 1),
        "ice_mask": plant((jax.random.randint(key_of[5], (NX, NY), 0, 10) < 9).astype(jnp.int32), jax.random.fold_in(key_of[5], 1), 0, 1),
        "driving": bell_draw(key_of[6], (2, NX, NY), 2.0, 8.0, ((1, 8),), jnp.float32),
        "obs_cell": plant(jax.random.randint(key_of[7], (N_TILE, N_LAYER, N_TILE, BLOCK), 0, CX * NY), jax.random.fold_in(key_of[7], 1), 0, (CX * NY) - 1).astype(jnp.int32),
        "obs_east": bell_draw(key_of[8], (N_TILE, N_LAYER, N_TILE, BLOCK), 1.0, 6.0, ((0, 8), (1, 4)), jnp.float32),
        "obs_north": bell_draw(key_of[9], (N_TILE, N_LAYER, N_TILE, BLOCK), 1.0, 6.0, ((0, 8), (1, 4)), jnp.float32),
        "obs_weight": jnp.clip(jnp.exp(math.log(1.0) - 2.3025851 * jax.random.uniform(key_of[10], (N_TILE, N_LAYER, N_TILE, BLOCK), jnp.float32) ** levels(key_of[10], (N_TILE, N_LAYER, N_TILE, BLOCK), ((0, 8), (1, 4)), -0.2, 0.2)), 0.1, 1.0),
        "obs_count": draw_obs_count(jax.random.fold_in(key_of[12], 71), 0),
    }


OMEGA = 0.5
REGULAR = 0.01


def pad_cols(field):
    return jnp.pad(field, ((0, 0), (1, 1)))


def pad_rows(field):
    return jnp.pad(field, ((1, 1), (0, 0)))


def col_diff(field):
    wide = pad_cols(field)
    return 0.5 * (wide[:, 2:] - wide[:, :-2])


def row_diff(field):
    return 0.5 * (field[2:] - field[:-2])


def strain_rate(east_vel, north_vel):
    slope_ux = row_diff(east_vel)
    slope_vx = row_diff(north_vel)
    slope_uy = col_diff(east_vel[1:-1])
    slope_vy = col_diff(north_vel[1:-1])
    shear = slope_uy + slope_vx
    return slope_ux * slope_ux + slope_vy * slope_vy + slope_ux * slope_vy + 0.25 * shear * shear + REGULAR


def sweep(east_vel, north_vel, viscous, force_east, force_north, drag, inside):
    centre_visc = viscous[1:-1]
    wide_visc = pad_cols(centre_visc)
    face_north = 0.5 * (centre_visc + viscous[2:])
    face_south = 0.5 * (centre_visc + viscous[:-2])
    face_east = 0.5 * (centre_visc + wide_visc[:, 2:])
    face_west = 0.5 * (centre_visc + wide_visc[:, :-2])
    drag_mid = drag[1:-1]
    inside_mid = inside[1:-1]

    def laplace(field, row_gain, col_gain):
        centre = field[1:-1]
        wide = pad_cols(centre)
        rows_part = face_north * (centre - field[2:]) + face_south * (centre - field[:-2])
        cols_part = face_east * (centre - wide[:, 2:]) + face_west * (centre - wide[:, :-2])
        return row_gain * rows_part + col_gain * cols_part + drag_mid * centre

    cross_east = row_diff(2.0 * viscous * col_diff(north_vel)) + col_diff(centre_visc * row_diff(north_vel))
    cross_north = col_diff(2.0 * centre_visc * row_diff(east_vel)) + row_diff(viscous * col_diff(east_vel))
    resid_east = force_east[1:-1] - (laplace(east_vel, 4.0, 1.0) - cross_east)
    resid_north = force_north[1:-1] - (laplace(north_vel, 1.0, 4.0) - cross_north)
    diag_east = 4.0 * (face_north + face_south) + face_east + face_west + drag_mid + 1.0 - inside_mid
    diag_north = face_north + face_south + 4.0 * (face_east + face_west) + drag_mid + 1.0 - inside_mid
    new_east = inside_mid * (east_vel[1:-1] + OMEGA * resid_east / diag_east)
    new_north = inside_mid * (north_vel[1:-1] + OMEGA * resid_north / diag_north)
    return new_east, new_north


def relax_full(start, forces, viscous, drag, inside):
    visc_pad = pad_rows(viscous)
    drag_pad = pad_rows(drag)
    inside_pad = pad_rows(inside)
    east_force = pad_rows(forces[0])
    north_force = pad_rows(forces[1])

    def one_sweep(step, fields):
        new_east, new_north = sweep(pad_rows(fields[0]), pad_rows(fields[1]), visc_pad, east_force, north_force, drag_pad, inside_pad)
        return jnp.stack([new_east, new_north], 0)

    return lax.fori_loop(0, SWEEPS, one_sweep, start)


def reference(velocity_guess, hardness, thickness, friction, grounded, ice_mask, driving, obs_cell, obs_east, obs_north, obs_weight, obs_count):
    strain = strain_rate(pad_rows(velocity_guess[0]), pad_rows(velocity_guess[1]))
    rate = jnp.power(strain, -1.0 / 3.0)
    viscous = thickness * (0.5 * rate * jnp.sum(hardness, axis=0)) / LAYERS
    drag = friction * grounded.astype(jnp.float32)
    inside = ice_mask.astype(jnp.float32)
    velocity = relax_full(velocity_guess, driving, viscous, drag, inside)
    slots = jnp.arange(BLOCK, dtype=jnp.int32)[None, None, None, :]
    valid = (slots < obs_count[..., None]).astype(jnp.float32)
    weights = (obs_weight * valid).reshape(-1)
    dest = jnp.arange(N_TILE, dtype=jnp.int32)[None, None, :, None]
    cells = (dest * (CX * NY) + obs_cell).reshape(-1).astype(jnp.int32)
    flat_east = velocity[0].reshape(-1)
    flat_north = velocity[1].reshape(-1)
    term_east = weights * (flat_east[cells] - obs_east.reshape(-1))
    term_north = weights * (flat_north[cells] - obs_north.reshape(-1))
    misfit_east = jax.ops.segment_sum(term_east, cells, num_segments=NX * NY).reshape(NX, NY)
    misfit_north = jax.ops.segment_sum(term_north, cells, num_segments=NX * NY).reshape(NX, NY)
    source = jnp.stack([misfit_east, misfit_north], 0)
    adjoint = relax_full(jnp.zeros_like(source), source, viscous, drag, inside)
    gradient = -(drag * (velocity[0] * adjoint[0] + velocity[1] * adjoint[1]))
    return velocity, gradient
```

```python
import functools

import jax
import jax.numpy as jnp
from jax import lax
from jax.experimental import pallas as pl
from jax.experimental.pallas import tpu as pltpu
from jax.sharding import PartitionSpec as P

SWEEPS = 40
OMEGA = 0.5
REGULAR = 0.01
HALO = 2 * SWEEPS
WIN = 256
LANES = 128
OFF = LANES - HALO
VMEM_LIMIT = 48 * 1024 * 1024


def scatter_maps(cell, east, north, weight, acc_ref, cols, first):
    blocks = cols // WIN
    slots = cell.shape[1]
    row = jnp.zeros_like(cell)
    for r in range(1, 8):
        row = row + jnp.where(cell >= r * cols, 1, 0)
    rem = cell - row * cols
    high = (rem // WIN) * 8 + row
    low = rem % WIN
    hit = lax.broadcasted_iota(jnp.int32, (8 * blocks, slots), 0) == high
    terms = []
    for value in (weight, weight * east, weight * north):
        rest = value
        for _ in range(3):
            part = rest.astype(jnp.bfloat16).astype(jnp.float32)
            rest = rest - part
            terms.append(jnp.where(hit, part, 0.0).astype(jnp.bfloat16))
    lhs = jnp.concatenate(terms, axis=0)
    rhs = jnp.where(
        lax.broadcasted_iota(jnp.int32, (WIN, slots), 0) == low, 1.0, 0.0
    ).astype(jnp.bfloat16)
    prod = lax.dot_general(
        lhs, rhs, (((1,), (1,)), ((), ())), preferred_element_type=jnp.float32
    )
    if first:
        acc_ref[...] = prod
    else:
        acc_ref[...] += prod


def maps_kernel(arr_ref, hard_ref, thick_ref, out_ref, acc_ref):
    cols = thick_ref.shape[1]
    blocks = cols // WIN
    hard = hard_ref[0]
    for k in range(1, hard_ref.shape[0]):
        hard = hard + hard_ref[k]
    out_ref[0] = hard * thick_ref[...]
    for s in range(arr_ref.shape[0]):
        scatter_maps(
            arr_ref[s, 0:1].astype(jnp.int32),
            arr_ref[s, 1:2],
            arr_ref[s, 2:3],
            arr_ref[s, 3:4],
            acc_ref,
            cols,
            s == 0,
        )
    n = 8 * blocks
    for v in range(3):
        for c in range(blocks):
            at = 3 * v * n + 8 * c
            out_ref[1 + v, :, c * WIN : (c + 1) * WIN] = (
                acc_ref[at : at + 8] + acc_ref[at + n : at + n + 8] + acc_ref[at + 2 * n : at + 2 * n + 8]
            )


def east_of(x):
    return pltpu.roll(x, WIN - 1, 1)


def west_of(x):
    return pltpu.roll(x, 1, 1)


def up(x):
    return pltpu.roll(x, x.shape[0] - 1, 0)


def down(x):
    return pltpu.roll(x, 1, 0)


def run_sweeps(state, coef, force):
    def wide(x):
        return (x, east_of(x), west_of(x))

    def rows(slot, a):
        return (wide(state[slot, 0, a]), wide(state[slot, 1, a]))

    def one(src, dst):
        first = rows(src, 0)
        last_u, last_v = state[src, 0, 7], state[src, 1, 7]
        before = (wide(down(last_u)), wide(down(last_v)))
        here = first
        for a in range(8):
            if a < 7:
                after = rows(src, a + 1)
            else:
                after = (wide(up(state[src, 0, 0])), wide(up(state[src, 1, 0])))
            for f in range(2):
                g = 1 - f
                c = lambda k: coef[f, k, a]
                new = c(0) * here[f][0] + force[f, a]
                new = new + c(1) * after[f][0]
                new = new + c(2) * before[f][0]
                new = new + c(3) * here[f][1]
                new = new + c(4) * here[f][2]
                new = new + c(5) * after[g][1]
                new = new + c(6) * after[g][2]
                new = new + c(7) * before[g][1]
                new = new + c(8) * before[g][2]
                state[dst, f, a] = new
            before, here = here, after

    def two(step, carry):
        one(0, 1)
        one(1, 0)
        return carry

    lax.fori_loop(0, SWEEPS // 2, two, 0)


def solve_kernel(layers, get, put, state, coef, gain, force):
    strips = state.shape[3]
    index = lax.broadcasted_iota(jnp.int32, (strips, WIN), 0)
    not_top = jnp.where(index == strips - 1, 0.0, 1.0)
    not_low = jnp.where(index == 0, 0.0, 1.0)

    def north(x, a):
        return x[a + 1] if a < 7 else up(x[0]) * not_top

    def south(x, a):
        return x[a - 1] if a > 0 else down(x[7]) * not_low

    u = [get(0, a) for a in range(8)]
    v = [get(1, a) for a in range(8)]
    visc = []
    for a in range(8):
        ux = 0.5 * (north(u, a) - south(u, a))
        vx = 0.5 * (north(v, a) - south(v, a))
        uy = 0.5 * (east_of(u[a]) - west_of(u[a]))
        vy = 0.5 * (east_of(v[a]) - west_of(v[a]))
        shear = uy + vx
        strain = ux * ux + vy * vy + ux * vy + 0.25 * shear * shear + REGULAR
        rate = jnp.exp(jnp.log(strain) * (-1.0 / 3.0))
        visc.append(0.5 * rate * get(6, a) / layers)
        state[0, 0, a] = u[a]
        state[0, 1, a] = v[a]
    for a in range(8):
        here = visc[a]
        vn, vs, ve, vw = north(visc, a), south(visc, a), east_of(here), west_of(here)
        fn, fs, fe, fw = (0.5 * (here + x) for x in (vn, vs, ve, vw))
        drag, inside = get(2, a), get(3, a)
        top = not_top if a == 7 else 1.0
        low = not_low if a == 0 else 1.0
        for f in range(2):
            rg, cg = (4.0, 1.0) if f == 0 else (1.0, 4.0)
            rx, cx = (0.5, 0.25) if f == 0 else (0.25, 0.5)
            spread = rg * (fn + fs) + cg * (fe + fw) + drag
            g = OMEGA * inside / (spread + 1.0 - inside)
            coef[f, 0, a] = inside - g * spread
            coef[f, 1, a] = g * rg * fn * top
            coef[f, 2, a] = g * rg * fs * low
            coef[f, 3, a] = g * cg * fe
            coef[f, 4, a] = g * cg * fw
            coef[f, 5, a] = g * (rx * vn + cx * ve) * top
            coef[f, 6, a] = -g * (rx * vn + cx * vw) * top
            coef[f, 7, a] = -g * (rx * vs + cx * ve) * low
            coef[f, 8, a] = g * (rx * vs + cx * vw) * low
            gain[f, a] = g
            force[f, a] = g * get(4 + f, a)
    run_sweeps(state, coef, force)
    for a in range(8):
        for f in range(2):
            vel = state[0, f, a]
            put(f, a, vel)
            force[f, a] = gain[f, a] * (vel * get(7, a) - get(8 + f, a))
            gain[f, a] = vel
            state[0, f, a] = jnp.zeros_like(vel)
    run_sweeps(state, coef, force)
    for a in range(8):
        put(2, a, -(get(2, a) * (gain[0, a] * state[0, 0, a] + gain[1, a] * state[0, 1, a])))


def solve_call(layers, x_ref, out_ref, state, coef, gain, force):
    def get(f, a):
        return x_ref[f, a]

    def put(f, a, value):
        out_ref[f, a] = pltpu.roll(value, WIN - HALO, 1)[:, :LANES]

    solve_kernel(layers, get, put, state, coef, gain, force)


def on_device(
    velocity_guess,
    hardness,
    thickness,
    friction,
    grounded,
    ice_mask,
    driving,
    obs_cell,
    obs_east,
    obs_north,
    obs_weight,
    obs_count,
):
    strips, parts = lax.axis_size("tile"), lax.axis_size("layer")
    cols = thickness.shape[1]
    group = cols // parts
    own = group // strips
    span = -(-(OFF + own * (strips - 1) + WIN) // LANES) * LANES
    layer = lax.axis_index("layer")
    drag = friction * grounded.astype(jnp.float32)
    inside = ice_mask.astype(jnp.float32)
    valid = (lax.broadcasted_iota(jnp.int32, obs_weight.shape, 3) < obs_count[..., None]).astype(
        jnp.float32
    )
    packed = jnp.stack(
        [obs_cell.astype(jnp.float32), obs_east, obs_north, obs_weight * valid], 0
    )[:, 0, 0]
    arrived = lax.all_to_all(packed.swapaxes(0, 1), "tile", split_axis=0, concat_axis=0, tiled=True)
    maps = pl.pallas_call(
        maps_kernel,
        out_shape=jax.ShapeDtypeStruct((4, 8, cols), jnp.float32),
        scratch_shapes=[pltpu.VMEM((9 * 8 * (cols // WIN), WIN), jnp.float32)],
        compiler_params=pltpu.CompilerParams(vmem_limit_bytes=VMEM_LIMIT),
    )(arrived, hardness, thickness)
    right = (parts - 1) * group + span - LANES - cols

    def pad(x):
        return jnp.pad(x, ((0, 0), (0, 0), (LANES, right)))

    def windows(x):
        return jnp.stack([x[:, :, OFF + own * t : OFF + own * t + WIN] for t in range(strips)], 0)

    maps = pad(maps)
    shares = jnp.stack([maps[:, :, group * p : group * p + span] for p in range(parts)], 0)
    summed = lax.psum_scatter(shares, "layer", scatter_dimension=0, tiled=False)
    plain = pad(jnp.concatenate([velocity_guess, drag[None], inside[None], driving], 0))
    plain = lax.dynamic_slice_in_dim(plain, layer * group, span, axis=2)
    send = windows(jnp.concatenate([plain, summed], 0))
    got = lax.all_to_all(send, "tile", split_axis=0, concat_axis=0, tiled=True)
    block = got.transpose(1, 2, 0, 3)
    result = pl.pallas_call(
        functools.partial(solve_call, float(hardness.shape[0] * parts)),
        out_shape=jax.ShapeDtypeStruct((3, 8, strips, LANES), jnp.float32),
        scratch_shapes=[
            pltpu.VMEM((2, 2, 8, strips, WIN), jnp.float32),
            pltpu.VMEM((2, 9, 8, strips, WIN), jnp.float32),
            pltpu.VMEM((2, 8, strips, WIN), jnp.float32),
            pltpu.VMEM((2, 8, strips, WIN), jnp.float32),
        ],
        compiler_params=pltpu.CompilerParams(vmem_limit_bytes=VMEM_LIMIT),
    )(block)
    back = lax.all_to_all(result.transpose(2, 0, 1, 3), "tile", split_axis=0, concat_axis=0, tiled=True)
    mine = back[..., :own].transpose(1, 2, 0, 3).reshape(3, 8, group)
    full = lax.all_gather(mine, "layer", axis=2, tiled=True)
    return full[:2], full[2]


def solution(mesh):
    return jax.shard_map(
        on_device,
        mesh=mesh,
        in_specs=(
            P(None, "tile", None),
            P("layer", "tile", None),
            P("tile", None),
            P("tile", None),
            P("tile", None),
            P("tile", None),
            P(None, "tile", None),
            P("tile", "layer", None, None),
            P("tile", "layer", None, None),
            P("tile", "layer", None, None),
            P("tile", "layer", None, None),
            P("tile", "layer", None),
        ),
        out_specs=(P(None, "tile", None), P("tile", None)),
        check_vma=False,
    )
```

```python
import functools

import jax
import jax.numpy as jnp
from jax import lax
from jax.experimental import pallas as pl
from jax.experimental.pallas import tpu as pltpu
from jax.sharding import PartitionSpec as P

SWEEPS = 40
OMEGA = 0.5
REGULAR = 0.01
HALO = 2 * SWEEPS
WIN = 256
LANES = 128
OFF = LANES - HALO
VMEM_LIMIT = 48 * 1024 * 1024


def scatter_maps(cell, east, north, weight, acc_ref, cols, first):
    blocks = cols // WIN
    slots = cell.shape[1]
    row = jnp.zeros_like(cell)
    for r in range(1, 8):
        row = row + jnp.where(cell >= r * cols, 1, 0)
    rem = cell - row * cols
    high = (rem // WIN) * 8 + row
    low = rem % WIN
    hit = lax.broadcasted_iota(jnp.int32, (8 * blocks, slots), 0) == high
    terms = []
    for value in (weight, weight * east, weight * north):
        rest = value
        for _ in range(3):
            part = rest.astype(jnp.bfloat16).astype(jnp.float32)
            rest = rest - part
            terms.append(jnp.where(hit, part, 0.0).astype(jnp.bfloat16))
    lhs = jnp.concatenate(terms, axis=0)
    rhs = jnp.where(
        lax.broadcasted_iota(jnp.int32, (WIN, slots), 0) == low, 1.0, 0.0
    ).astype(jnp.bfloat16)
    prod = lax.dot_general(
        lhs, rhs, (((1,), (1,)), ((), ())), preferred_element_type=jnp.float32
    )
    if first:
        acc_ref[...] = prod
    else:
        acc_ref[...] += prod


def east_of(x):
    return pltpu.roll(x, WIN - 1, 1)


def west_of(x):
    return pltpu.roll(x, 1, 1)


def up(x):
    return pltpu.roll(x, x.shape[0] - 1, 0)


def down(x):
    return pltpu.roll(x, 1, 0)


def run_sweeps(state, coef, force, count):
    def wide(x):
        return (x, east_of(x), west_of(x))

    def rows(slot, a):
        return (wide(state[slot, 0, a]), wide(state[slot, 1, a]))

    def one(src, dst):
        first = rows(src, 0)
        last_u, last_v = state[src, 0, 7], state[src, 1, 7]
        before = (wide(down(last_u)), wide(down(last_v)))
        here = first
        for a in range(8):
            if a < 7:
                after = rows(src, a + 1)
            else:
                after = (wide(up(state[src, 0, 0])), wide(up(state[src, 1, 0])))
            for f in range(2):
                g = 1 - f
                c = lambda k: coef[f, k, a]
                new = c(0) * here[f][0] + force[f, a]
                new = new + c(1) * after[f][0]
                new = new + c(2) * before[f][0]
                new = new + c(3) * here[f][1]
                new = new + c(4) * here[f][2]
                new = new + c(5) * after[g][1]
                new = new + c(6) * after[g][2]
                new = new + c(7) * before[g][1]
                new = new + c(8) * before[g][2]
                state[dst, f, a] = new
            before, here = here, after

    def two(step, carry):
        one(0, 1)
        one(1, 0)
        return carry

    lax.fori_loop(0, count // 2, two, 0)


def make_coefs(layers, get, state, coef, gain, force):
    strips = state.shape[3]
    index = lax.broadcasted_iota(jnp.int32, (strips, WIN), 0)
    not_top = jnp.where(index == strips - 1, 0.0, 1.0)
    not_low = jnp.where(index == 0, 0.0, 1.0)

    def north(x, a):
        return x[a + 1] if a < 7 else up(x[0]) * not_top

    def south(x, a):
        return x[a - 1] if a > 0 else down(x[7]) * not_low

    u = [get(0, a) for a in range(8)]
    v = [get(1, a) for a in range(8)]
    visc = []
    for a in range(8):
        ux = 0.5 * (north(u, a) - south(u, a))
        vx = 0.5 * (north(v, a) - south(v, a))
        uy = 0.5 * (east_of(u[a]) - west_of(u[a]))
        vy = 0.5 * (east_of(v[a]) - west_of(v[a]))
        shear = uy + vx
        strain = ux * ux + vy * vy + ux * vy + 0.25 * shear * shear + REGULAR
        rate = jnp.exp(jnp.log(strain) * (-1.0 / 3.0))
        visc.append(0.5 * rate * get(6, a) / layers)
        state[0, 0, a] = u[a]
        state[0, 1, a] = v[a]
    for a in range(8):
        here = visc[a]
        vn, vs, ve, vw = north(visc, a), south(visc, a), east_of(here), west_of(here)
        fn, fs, fe, fw = (0.5 * (here + x) for x in (vn, vs, ve, vw))
        drag, inside = get(2, a), get(3, a)
        top = not_top if a == 7 else 1.0
        low = not_low if a == 0 else 1.0
        for f in range(2):
            rg, cg = (4.0, 1.0) if f == 0 else (1.0, 4.0)
            rx, cx = (0.5, 0.25) if f == 0 else (0.25, 0.5)
            spread = rg * (fn + fs) + cg * (fe + fw) + drag
            g = OMEGA * inside / (spread + 1.0 - inside)
            coef[f, 0, a] = inside - g * spread
            coef[f, 1, a] = g * rg * fn * top
            coef[f, 2, a] = g * rg * fs * low
            coef[f, 3, a] = g * cg * fe
            coef[f, 4, a] = g * cg * fw
            coef[f, 5, a] = g * (rx * vn + cx * ve) * top
            coef[f, 6, a] = -g * (rx * vn + cx * vw) * top
            coef[f, 7, a] = -g * (rx * vs + cx * ve) * low
            coef[f, 8, a] = g * (rx * vs + cx * vw) * low
            gain[f, a] = g
            force[f, a] = g * get(4 + f, a)


MESH = pl.DeviceIdType.MESH
EARLY = 16


def exchange(axis, peers, source, target, send_sem, recv_sem):
    copies = []
    for k, peer in enumerate(peers):
        copy = pltpu.make_async_remote_copy(
            src_ref=source(k, peer),
            dst_ref=target(k),
            send_sem=send_sem.at[k],
            recv_sem=recv_sem.at[k],
            device_id={axis: peer},
            device_id_type=MESH,
        )
        copy.start()
        copies.append(copy)
    return copies


def finish(copies):
    for copy in copies:
        copy.wait()


def cut_window(tiles, own, t):
    at = OFF + own * t
    first, skip = at // LANES, at % LANES
    if skip == 0:
        return jnp.concatenate([tiles[first], tiles[first + 1]], axis=1)
    keep = lax.broadcasted_iota(jnp.int32, (8, LANES), 1) < LANES - skip
    turned = [pltpu.roll(tiles[first + j], LANES - skip, 1) for j in range(3)]
    return jnp.concatenate(
        [jnp.where(keep, turned[j], turned[j + 1]) for j in range(2)], axis=1
    )


def join_pieces(pieces, own, q):
    lane = lax.broadcasted_iota(jnp.int32, (8, LANES), 1)
    tile = None
    for s, piece in enumerate(pieces):
        shift = own * s - LANES * q
        if shift + own <= 0 or shift >= LANES:
            continue
        moved = piece if shift % LANES == 0 else pltpu.roll(piece, shift % LANES, 1)
        tile = moved if tile is None else jnp.where(lane >= shift, moved, tile)
    return tile


def fused_kernel(
    strips,
    parts,
    guess_ref,
    hard_ref,
    thick_ref,
    fric_ref,
    ground_ref,
    mask_ref,
    drive_ref,
    cell_ref,
    east_ref,
    north_ref,
    weight_ref,
    count_ref,
    vel_ref,
    grad_ref,
    obs_out,
    obs_in,
    hard_buf,
    hard_in,
    maps_buf,
    maps_in,
    acc_ref,
    send_a,
    recv_a,
    send_b,
    recv_b,
    send_c,
    recv_c,
    x_ref,
    state,
    coef,
    gain,
    force,
    vel_out,
    vel_in,
    vel_all,
    grad_out,
    grad_in,
    grad_all,
    tile_send,
    tile_recv,
    layer_send,
    layer_recv,
):
    cols = thick_ref.shape[1]
    group = cols // parts
    own = group // strips
    step = group // LANES
    span = hard_in.shape[1]
    layers = float(hard_ref.shape[0] * parts)
    me, layer = lax.axis_index("tile"), lax.axis_index("layer")
    others = [lax.rem(me + k, strips) for k in range(1, strips)]
    mates = [lax.rem(layer + k, parts) for k in range(1, parts)]

    barrier = pltpu.get_barrier_semaphore()
    for peer in others:
        pl.semaphore_signal(barrier, inc=1, device_id={"tile": peer}, device_id_type=MESH)
    for peer in mates:
        pl.semaphore_signal(barrier, inc=1, device_id={"layer": peer}, device_id_type=MESH)

    zero = jnp.zeros((8, LANES), jnp.float32)
    total = hard_buf.shape[0]
    for i in range(total):
        at = (i - 1) * LANES
        if 0 <= at < cols:
            value = hard_ref[0, :, at : at + LANES]
            for k in range(1, hard_ref.shape[0]):
                value = value + hard_ref[k, :, at : at + LANES]
            hard_buf[i] = value * thick_ref[:, at : at + LANES]
        else:
            hard_buf[i] = zero
            for f in range(3):
                maps_buf[f, i] = zero
    slot = lax.broadcasted_iota(jnp.int32, (1, cell_ref.shape[3]), 1)
    for d in range(strips):
        obs_out[d, 0:1] = cell_ref[0, 0, d : d + 1].astype(jnp.float32)
        obs_out[d, 1:2] = east_ref[0, 0, d : d + 1]
        obs_out[d, 2:3] = north_ref[0, 0, d : d + 1]
        obs_out[d, 3:4] = jnp.where(slot < count_ref[0, 0, d], weight_ref[0, 0, d : d + 1], 0.0)

    def group_tiles(load):
        tiles = []
        for i in range(span):
            at = group * layer + (i - 1) * LANES
            if 1 <= i <= step:
                tiles.append(load(pl.ds(pl.multiple_of(at, LANES), LANES)))
            else:
                inside = jnp.logical_and(at >= 0, at < cols)
                safe = jnp.where(inside, at, 0)
                value = load(pl.ds(pl.multiple_of(safe, LANES), LANES))
                tiles.append(jnp.where(inside, value, 0.0))
        return tiles

    loads = [
        lambda at: guess_ref[0, :, at],
        lambda at: guess_ref[1, :, at],
        lambda at: fric_ref[:, at] * ground_ref[:, at].astype(jnp.float32),
        lambda at: mask_ref[:, at].astype(jnp.float32),
        lambda at: drive_ref[0, :, at],
        lambda at: drive_ref[1, :, at],
    ]
    for f, load in enumerate(loads):
        tiles = group_tiles(load)
        for t in range(strips):
            send_a[t, f] = cut_window(tiles, own, t)

    def tile_exchange(n, out, into):
        return exchange(
            "tile",
            others,
            lambda k, peer: out.at[peer],
            lambda k: into.at[me],
            tile_send.at[n],
            tile_recv.at[n],
        )

    pl.semaphore_wait(barrier, strips + parts - 2)
    hard_copies = exchange(
        "layer",
        mates,
        lambda k, peer: hard_buf.at[pl.ds(step * peer, span)],
        lambda k: hard_in.at[k],
        layer_send.at[0],
        layer_recv.at[0],
    )
    obs_copies = tile_exchange(0, obs_out, obs_in)
    a_copies = tile_exchange(1, send_a, recv_a)
    obs_in[me] = obs_out[me]
    recv_a[me] = send_a[me]

    finish(hard_copies)
    tiles = []
    for i in range(span):
        value = hard_buf[step * layer + i]
        for k in range(parts - 1):
            value = value + hard_in[k, i]
        tiles.append(value)
    for t in range(strips):
        send_b[t] = cut_window(tiles, own, t)
    b_copies = tile_exchange(2, send_b, recv_b)
    recv_b[me] = send_b[me]

    finish(obs_copies)
    for s in range(strips):
        scatter_maps(
            obs_in[s, 0:1].astype(jnp.int32),
            obs_in[s, 1:2],
            obs_in[s, 2:3],
            obs_in[s, 3:4],
            acc_ref,
            cols,
            s == 0,
        )
    n = 8 * (cols // WIN)
    for f in range(3):
        for i in range(cols // LANES):
            at = 3 * f * n + 8 * (i // 2)
            half = slice((i % 2) * LANES, (i % 2 + 1) * LANES)
            maps_buf[f, i + 1] = (
                acc_ref[at : at + 8, half]
                + acc_ref[at + n : at + n + 8, half]
                + acc_ref[at + 2 * n : at + 2 * n + 8, half]
            )
    maps_copies = exchange(
        "layer",
        mates,
        lambda k, peer: maps_buf.at[:, pl.ds(step * peer, span)],
        lambda k: maps_in.at[k],
        layer_send.at[1],
        layer_recv.at[1],
    )

    finish(a_copies)
    finish(b_copies)
    for f in range(6):
        x_ref[f] = jnp.swapaxes(recv_a[:, f], 0, 1)
    x_ref[6] = jnp.swapaxes(recv_b[...], 0, 1)

    def get(f, a):
        return x_ref[f, a]

    make_coefs(layers, get, state, coef, gain, force)
    run_sweeps(state, coef, force, EARLY)

    finish(maps_copies)
    for f in range(3):
        tiles = []
        for i in range(span):
            value = maps_buf[f, step * layer + i]
            for k in range(parts - 1):
                value = value + maps_in[k, f, i]
            tiles.append(value)
        for t in range(strips):
            send_c[t, f] = cut_window(tiles, own, t)
    c_copies = tile_exchange(3, send_c, recv_c)
    recv_c[me] = send_c[me]
    run_sweeps(state, coef, force, SWEEPS - EARLY)

    def own_part(value):
        return pltpu.roll(value, WIN - HALO, 1)[:, :LANES]

    for f in range(2):
        parts_f = jnp.stack([own_part(state[0, f, a]) for a in range(8)], 0)
        vel_out[:, f] = jnp.swapaxes(parts_f, 0, 1)
    vel_copies = tile_exchange(4, vel_out, vel_in)
    vel_in[me] = vel_out[me]

    finish(c_copies)
    for f in range(3):
        x_ref[7 + f] = jnp.swapaxes(recv_c[:, f], 0, 1)
    for a in range(8):
        for f in range(2):
            vel = state[0, f, a]
            force[f, a] = gain[f, a] * (vel * get(7, a) - get(8 + f, a))
            gain[f, a] = vel
            state[0, f, a] = jnp.zeros_like(vel)
    run_sweeps(state, coef, force, EARLY)

    def layer_gather(n, every):
        here = every.at[:, pl.ds(step * layer, step)]
        return exchange(
            "layer", mates, lambda k, peer: here, lambda k: here, layer_send.at[n], layer_recv.at[n]
        )

    finish(vel_copies)
    for f in range(2):
        pieces = [vel_in[s, f] for s in range(strips)]
        for q in range(step):
            vel_all[f, step * layer + q] = join_pieces(pieces, own, q)
    gather_copies = layer_gather(2, vel_all)
    run_sweeps(state, coef, force, SWEEPS - EARLY)

    rows = jnp.stack(
        [
            own_part(
                -(get(2, a) * (gain[0, a] * state[0, 0, a] + gain[1, a] * state[0, 1, a]))
            )
            for a in range(8)
        ],
        0,
    )
    grad_out[...] = jnp.swapaxes(rows, 0, 1)
    grad_copies = tile_exchange(5, grad_out, grad_in)
    grad_in[me] = grad_out[me]
    finish(gather_copies)
    for f in range(2):
        for i in range(cols // LANES):
            vel_ref[f, :, i * LANES : (i + 1) * LANES] = vel_all[f, i]
    finish(grad_copies)
    pieces = [grad_in[s] for s in range(strips)]
    for q in range(step):
        grad_all[0, step * layer + q] = join_pieces(pieces, own, q)
    finish(layer_gather(3, grad_all))
    for i in range(cols // LANES):
        grad_ref[:, i * LANES : (i + 1) * LANES] = grad_all[0, i]


def on_device(*fields):
    strips, parts = lax.axis_size("tile"), lax.axis_size("layer")
    cols = fields[2].shape[1]
    slots = fields[7].shape[3]
    group = cols // parts
    own = group // strips
    span = -(-(OFF + own * (strips - 1) + WIN) // LANES)
    total = group // LANES * (parts - 1) + span
    tiles = cols // LANES

    def vmem(*shape):
        return pltpu.VMEM(shape, jnp.float32)

    in_specs = [pl.BlockSpec(memory_space=pltpu.VMEM)] * 11
    in_specs.append(pl.BlockSpec(memory_space=pltpu.SMEM))
    return pl.pallas_call(
        functools.partial(fused_kernel, strips, parts),
        out_shape=(
            jax.ShapeDtypeStruct((2, 8, cols), jnp.float32),
            jax.ShapeDtypeStruct((8, cols), jnp.float32),
        ),
        in_specs=in_specs,
        out_specs=(pl.BlockSpec(memory_space=pltpu.VMEM),) * 2,
        scratch_shapes=[
            vmem(strips, 4, slots),
            vmem(strips, 4, slots),
            vmem(total, 8, LANES),
            vmem(parts - 1, span, 8, LANES),
            vmem(3, total, 8, LANES),
            vmem(parts - 1, 3, span, 8, LANES),
            vmem(9 * 8 * (cols // WIN), WIN),
            vmem(strips, 6, 8, WIN),
            vmem(strips, 6, 8, WIN),
            vmem(strips, 8, WIN),
            vmem(strips, 8, WIN),
            vmem(strips, 3, 8, WIN),
            vmem(strips, 3, 8, WIN),
            vmem(10, 8, strips, WIN),
            vmem(2, 2, 8, strips, WIN),
            vmem(2, 9, 8, strips, WIN),
            vmem(2, 8, strips, WIN),
            vmem(2, 8, strips, WIN),
            vmem(strips, 2, 8, LANES),
            vmem(strips, 2, 8, LANES),
            vmem(2, tiles, 8, LANES),
            vmem(strips, 8, LANES),
            vmem(strips, 8, LANES),
            vmem(1, tiles, 8, LANES),
            pltpu.SemaphoreType.DMA((6, strips - 1)),
            pltpu.SemaphoreType.DMA((6, strips - 1)),
            pltpu.SemaphoreType.DMA((4, parts - 1)),
            pltpu.SemaphoreType.DMA((4, parts - 1)),
        ],
        compiler_params=pltpu.CompilerParams(
            collective_id=0, has_side_effects=True, vmem_limit_bytes=VMEM_LIMIT
        ),
    )(*fields)


def solution(mesh):
    return jax.shard_map(
        on_device,
        mesh=mesh,
        in_specs=(
            P(None, "tile", None),
            P("layer", "tile", None),
            P("tile", None),
            P("tile", None),
            P("tile", None),
            P("tile", None),
            P(None, "tile", None),
            P("tile", "layer", None, None),
            P("tile", "layer", None, None),
            P("tile", "layer", None, None),
            P("tile", "layer", None, None),
            P("tile", "layer", None),
        ),
        out_specs=(P(None, "tile", None), P("tile", None)),
        check_vma=False,
    )
```

```python
import functools

import jax
import jax.numpy as jnp
from jax import lax
from jax.experimental import pallas as pl
from jax.experimental.pallas import tpu as pltpu
from jax.sharding import PartitionSpec as P

SWEEPS = 40
OMEGA = 0.5
REGULAR = 0.01
HALO = 2 * SWEEPS
WIN = 256
LANES = 128
OFF = LANES - HALO
VMEM_LIMIT = 60 * 1024 * 1024


def scatter_maps(cell, east, north, weight, acc_ref, cols, first):
    blocks = cols // WIN
    slots = cell.shape[1]
    row = jnp.zeros_like(cell)
    for r in range(1, 8):
        row = row + jnp.where(cell >= r * cols, 1, 0)
    rem = cell - row * cols
    high = (rem // WIN) * 8 + row
    low = rem % WIN
    hit = lax.broadcasted_iota(jnp.int32, (8 * blocks, slots), 0) == high
    terms = []
    for value in (weight, weight * east, weight * north):
        rest = value
        for _ in range(3):
            part = rest.astype(jnp.bfloat16).astype(jnp.float32)
            rest = rest - part
            terms.append(jnp.where(hit, part, 0.0).astype(jnp.bfloat16))
    lhs = jnp.concatenate(terms, axis=0)
    rhs = jnp.where(
        lax.broadcasted_iota(jnp.int32, (WIN, slots), 0) == low, 1.0, 0.0
    ).astype(jnp.bfloat16)
    prod = lax.dot_general(
        lhs, rhs, (((1,), (1,)), ((), ())), preferred_element_type=jnp.float32
    )
    if first:
        acc_ref[...] = prod
    else:
        acc_ref[...] += prod


def east_of(x):
    return pltpu.roll(x, WIN - 1, 1)


def west_of(x):
    return pltpu.roll(x, 1, 1)


def up(x):
    return pltpu.roll(x, x.shape[0] - 1, 0)


def down(x):
    return pltpu.roll(x, 1, 0)


def run_sweeps(state, coef, force, count):
    def wide(x):
        return (x, east_of(x), west_of(x))

    def rows(slot, a):
        return (wide(state[slot, 0, a]), wide(state[slot, 1, a]))

    def one(src, dst):
        first = rows(src, 0)
        last_u, last_v = state[src, 0, 7], state[src, 1, 7]
        before = (wide(down(last_u)), wide(down(last_v)))
        here = first
        for a in range(8):
            if a < 7:
                after = rows(src, a + 1)
            else:
                after = (wide(up(state[src, 0, 0])), wide(up(state[src, 1, 0])))
            for f in range(2):
                g = 1 - f
                c = lambda k: coef[f, k, a]
                new = c(0) * here[f][0] + force[f, a]
                new = new + c(1) * after[f][0]
                new = new + c(2) * before[f][0]
                new = new + c(3) * here[f][1]
                new = new + c(4) * here[f][2]
                new = new + c(5) * after[g][1]
                new = new + c(6) * after[g][2]
                new = new + c(7) * before[g][1]
                new = new + c(8) * before[g][2]
                state[dst, f, a] = new
            before, here = here, after

    def two(step, carry):
        one(0, 1)
        one(1, 0)
        return carry

    lax.fori_loop(0, count // 2, two, 0)


def make_coefs(layers, get, state, coef, gain, force):
    strips = state.shape[3]
    index = lax.broadcasted_iota(jnp.int32, (strips, WIN), 0)
    not_top = jnp.where(index == strips - 1, 0.0, 1.0)
    not_low = jnp.where(index == 0, 0.0, 1.0)

    def north(x, a):
        return x[a + 1] if a < 7 else up(x[0]) * not_top

    def south(x, a):
        return x[a - 1] if a > 0 else down(x[7]) * not_low

    u = [get(0, a) for a in range(8)]
    v = [get(1, a) for a in range(8)]
    visc = []
    for a in range(8):
        ux = 0.5 * (north(u, a) - south(u, a))
        vx = 0.5 * (north(v, a) - south(v, a))
        uy = 0.5 * (east_of(u[a]) - west_of(u[a]))
        vy = 0.5 * (east_of(v[a]) - west_of(v[a]))
        shear = uy + vx
        strain = ux * ux + vy * vy + ux * vy + 0.25 * shear * shear + REGULAR
        rate = jnp.exp(jnp.log(strain) * (-1.0 / 3.0))
        visc.append(0.5 * rate * get(6, a) / layers)
        state[0, 0, a] = u[a]
        state[0, 1, a] = v[a]
    for a in range(8):
        here = visc[a]
        vn, vs, ve, vw = north(visc, a), south(visc, a), east_of(here), west_of(here)
        fn, fs, fe, fw = (0.5 * (here + x) for x in (vn, vs, ve, vw))
        drag, inside = get(2, a), get(3, a)
        top = not_top if a == 7 else 1.0
        low = not_low if a == 0 else 1.0
        for f in range(2):
            rg, cg = (4.0, 1.0) if f == 0 else (1.0, 4.0)
            rx, cx = (0.5, 0.25) if f == 0 else (0.25, 0.5)
            spread = rg * (fn + fs) + cg * (fe + fw) + drag
            g = OMEGA * inside / (spread + 1.0 - inside)
            coef[f, 0, a] = inside - g * spread
            coef[f, 1, a] = g * rg * fn * top
            coef[f, 2, a] = g * rg * fs * low
            coef[f, 3, a] = g * cg * fe
            coef[f, 4, a] = g * cg * fw
            coef[f, 5, a] = g * (rx * vn + cx * ve) * top
            coef[f, 6, a] = -g * (rx * vn + cx * vw) * top
            coef[f, 7, a] = -g * (rx * vs + cx * ve) * low
            coef[f, 8, a] = g * (rx * vs + cx * vw) * low
            gain[f, a] = g
            force[f, a] = g * get(4 + f, a)


MESH = pl.DeviceIdType.MESH
EARLY = 4
RETURN = 16


def exchange(axis, peers, source, target, send_sem, recv_sem):
    copies = []
    for k, peer in enumerate(peers):
        copy = pltpu.make_async_remote_copy(
            src_ref=source(k, peer),
            dst_ref=target(k),
            send_sem=send_sem.at[k],
            recv_sem=recv_sem.at[k],
            device_id={axis: peer},
            device_id_type=MESH,
        )
        copy.start()
        copies.append(copy)
    return copies


def finish(copies):
    for copy in copies:
        copy.wait()


def cut_window(tiles, own, t):
    at = OFF + own * t
    first, skip = at // LANES, at % LANES
    if skip == 0:
        return jnp.concatenate([tiles[first], tiles[first + 1]], axis=1)
    keep = lax.broadcasted_iota(jnp.int32, (8, LANES), 1) < LANES - skip
    turned = [pltpu.roll(tiles[first + j], LANES - skip, 1) for j in range(3)]
    return jnp.concatenate(
        [jnp.where(keep, turned[j], turned[j + 1]) for j in range(2)], axis=1
    )


def join_pieces(pieces, own, q):
    lane = lax.broadcasted_iota(jnp.int32, (8, LANES), 1)
    tile = None
    for s, piece in enumerate(pieces):
        shift = own * s - LANES * q
        if shift + own <= 0 or shift >= LANES:
            continue
        moved = piece if shift % LANES == 0 else pltpu.roll(piece, shift % LANES, 1)
        tile = moved if tile is None else jnp.where(lane >= shift, moved, tile)
    return tile


def fused_kernel(
    strips,
    parts,
    *refs,
):
    args, (vel_ref, grad_ref), held = refs[:12], refs[12:14], refs[14:26]
    (
    obs_out,
    obs_in,
    hard_buf,
    hard_in,
    maps_buf,
    maps_in,
    acc_ref,
    send_a,
    recv_a,
    send_b,
    recv_b,
    send_c,
    recv_c,
    x_ref,
    state,
    coef,
    gain,
    force,
    vel_out,
    vel_in,
    vel_all,
    grad_out,
    grad_in,
    grad_all,
    tile_send,
    tile_recv,
    layer_send,
    layer_recv,
    load_sem,
    ) = refs[26:]
    (
        guess_ref,
        hard_ref,
        thick_ref,
        fric_ref,
        ground_ref,
        mask_ref,
        drive_ref,
        cell_ref,
        east_ref,
        north_ref,
        weight_ref,
        count_ref,
    ) = held
    cols = thick_ref.shape[1]
    group = cols // parts
    own = group // strips
    step = group // LANES
    span = hard_in.shape[1]
    layers = float(hard_ref.shape[0] * parts)
    me, layer = lax.axis_index("tile"), lax.axis_index("layer")
    others = [lax.rem(me + k, strips) for k in range(1, strips)]
    mates = [lax.rem(layer + k, parts) for k in range(1, parts)]

    barrier = pltpu.get_barrier_semaphore()
    for peer in others:
        pl.semaphore_signal(barrier, inc=1, device_id={"tile": peer}, device_id_type=MESH)
    for peer in mates:
        pl.semaphore_signal(barrier, inc=1, device_id={"layer": peer}, device_id_type=MESH)

    arrivals = [
        pltpu.make_async_copy(args[n], held[n], load_sem.at[n]) for n in range(len(args))
    ]
    for n in (7, 8, 9, 10, 11, 1, 2, 0, 3, 4, 5, 6):
        arrivals[n].start()

    for n in (1, 2):
        arrivals[n].wait()
    zero = jnp.zeros((8, LANES), jnp.float32)
    total = hard_buf.shape[0]
    for i in range(total):
        at = (i - 1) * LANES
        if 0 <= at < cols:
            value = hard_ref[0, :, at : at + LANES]
            for k in range(1, hard_ref.shape[0]):
                value = value + hard_ref[k, :, at : at + LANES]
            hard_buf[i] = value * thick_ref[:, at : at + LANES]
        else:
            hard_buf[i] = zero
            for f in range(3):
                maps_buf[f, i] = zero
    for n in (7, 8, 9, 10, 11):
        arrivals[n].wait()
    slot = lax.broadcasted_iota(jnp.int32, (1, cell_ref.shape[3]), 1)
    for d in range(strips):
        obs_out[d, 0:1] = cell_ref[0, 0, d : d + 1].astype(jnp.float32)
        obs_out[d, 1:2] = east_ref[0, 0, d : d + 1]
        obs_out[d, 2:3] = north_ref[0, 0, d : d + 1]
        obs_out[d, 3:4] = jnp.where(slot < count_ref[0, :, d : d + 1], weight_ref[0, 0, d : d + 1], 0.0)

    for n in (0, 3, 4, 5, 6):
        arrivals[n].wait()
    def group_tiles(load):
        tiles = []
        for i in range(span):
            at = group * layer + (i - 1) * LANES
            if 1 <= i <= step:
                tiles.append(load(pl.ds(pl.multiple_of(at, LANES), LANES)))
            else:
                inside = jnp.logical_and(at >= 0, at < cols)
                safe = jnp.where(inside, at, 0)
                value = load(pl.ds(pl.multiple_of(safe, LANES), LANES))
                tiles.append(jnp.where(inside, value, 0.0))
        return tiles

    loads = [
        lambda at: guess_ref[0, :, at],
        lambda at: guess_ref[1, :, at],
        lambda at: fric_ref[:, at] * ground_ref[:, at].astype(jnp.float32),
        lambda at: mask_ref[:, at].astype(jnp.float32),
        lambda at: drive_ref[0, :, at],
        lambda at: drive_ref[1, :, at],
    ]
    for f, load in enumerate(loads):
        tiles = group_tiles(load)
        for t in range(strips):
            send_a[t, f] = cut_window(tiles, own, t)

    def tile_exchange(n, out, into):
        return exchange(
            "tile",
            others,
            lambda k, peer: out.at[peer],
            lambda k: into.at[me],
            tile_send.at[n],
            tile_recv.at[n],
        )

    pl.semaphore_wait(barrier, strips + parts - 2)
    hard_copies = exchange(
        "layer",
        mates,
        lambda k, peer: hard_buf.at[pl.ds(step * peer, span)],
        lambda k: hard_in.at[k],
        layer_send.at[0],
        layer_recv.at[0],
    )
    obs_copies = tile_exchange(0, obs_out, obs_in)
    a_copies = tile_exchange(1, send_a, recv_a)
    obs_in[me] = obs_out[me]
    recv_a[me] = send_a[me]

    finish(hard_copies)
    tiles = []
    for i in range(span):
        value = hard_buf[step * layer + i]
        for k in range(parts - 1):
            value = value + hard_in[k, i]
        tiles.append(value)
    for t in range(strips):
        send_b[t] = cut_window(tiles, own, t)
    b_copies = tile_exchange(2, send_b, recv_b)
    recv_b[me] = send_b[me]

    finish(obs_copies)
    for s in range(strips):
        scatter_maps(
            obs_in[s, 0:1].astype(jnp.int32),
            obs_in[s, 1:2],
            obs_in[s, 2:3],
            obs_in[s, 3:4],
            acc_ref,
            cols,
            s == 0,
        )
    n = 8 * (cols // WIN)
    for f in range(3):
        for i in range(cols // LANES):
            at = 3 * f * n + 8 * (i // 2)
            half = slice((i % 2) * LANES, (i % 2 + 1) * LANES)
            maps_buf[f, i + 1] = (
                acc_ref[at : at + 8, half]
                + acc_ref[at + n : at + n + 8, half]
                + acc_ref[at + 2 * n : at + 2 * n + 8, half]
            )
    maps_copies = exchange(
        "layer",
        mates,
        lambda k, peer: maps_buf.at[:, pl.ds(step * peer, span)],
        lambda k: maps_in.at[k],
        layer_send.at[1],
        layer_recv.at[1],
    )

    finish(a_copies)
    finish(b_copies)
    for f in range(6):
        x_ref[f] = jnp.swapaxes(recv_a[:, f], 0, 1)
    x_ref[6] = jnp.swapaxes(recv_b[...], 0, 1)

    def get(f, a):
        return x_ref[f, a]

    make_coefs(layers, get, state, coef, gain, force)
    run_sweeps(state, coef, force, EARLY)

    finish(maps_copies)
    for f in range(3):
        tiles = []
        for i in range(span):
            value = maps_buf[f, step * layer + i]
            for k in range(parts - 1):
                value = value + maps_in[k, f, i]
            tiles.append(value)
        for t in range(strips):
            send_c[t, f] = cut_window(tiles, own, t)
    c_copies = tile_exchange(3, send_c, recv_c)
    recv_c[me] = send_c[me]
    run_sweeps(state, coef, force, SWEEPS - EARLY)

    def own_part(value):
        return pltpu.roll(value, WIN - HALO, 1)[:, :LANES]

    for f in range(2):
        parts_f = jnp.stack([own_part(state[0, f, a]) for a in range(8)], 0)
        vel_out[:, f] = jnp.swapaxes(parts_f, 0, 1)
    vel_copies = tile_exchange(4, vel_out, vel_in)
    vel_in[me] = vel_out[me]

    finish(c_copies)
    for f in range(3):
        x_ref[7 + f] = jnp.swapaxes(recv_c[:, f], 0, 1)
    for a in range(8):
        for f in range(2):
            vel = state[0, f, a]
            force[f, a] = gain[f, a] * (vel * get(7, a) - get(8 + f, a))
            gain[f, a] = vel
            state[0, f, a] = jnp.zeros_like(vel)
    run_sweeps(state, coef, force, RETURN)

    def layer_gather(n, every):
        here = every.at[:, pl.ds(step * layer, step)]
        return exchange(
            "layer", mates, lambda k, peer: here, lambda k: here, layer_send.at[n], layer_recv.at[n]
        )

    finish(vel_copies)
    for f in range(2):
        pieces = [vel_in[s, f] for s in range(strips)]
        for q in range(step):
            vel_all[f, step * layer + q] = join_pieces(pieces, own, q)
    gather_copies = layer_gather(2, vel_all)
    run_sweeps(state, coef, force, SWEEPS - RETURN)

    rows = jnp.stack(
        [
            own_part(
                -(get(2, a) * (gain[0, a] * state[0, 0, a] + gain[1, a] * state[0, 1, a]))
            )
            for a in range(8)
        ],
        0,
    )
    grad_out[...] = jnp.swapaxes(rows, 0, 1)
    grad_copies = tile_exchange(5, grad_out, grad_in)
    grad_in[me] = grad_out[me]
    finish(gather_copies)
    for f in range(2):
        for i in range(cols // LANES):
            vel_ref[f, :, i * LANES : (i + 1) * LANES] = vel_all[f, i]
    finish(grad_copies)
    pieces = [grad_in[s] for s in range(strips)]
    for q in range(step):
        grad_all[0, step * layer + q] = join_pieces(pieces, own, q)
    finish(layer_gather(3, grad_all))
    for i in range(cols // LANES):
        grad_ref[:, i * LANES : (i + 1) * LANES] = grad_all[0, i]


def on_device(*fields):
    strips, parts = lax.axis_size("tile"), lax.axis_size("layer")
    cols = fields[2].shape[1]
    slots = fields[7].shape[3]
    group = cols // parts
    own = group // strips
    span = -(-(OFF + own * (strips - 1) + WIN) // LANES)
    total = group // LANES * (parts - 1) + span
    tiles = cols // LANES

    def vmem(*shape):
        return pltpu.VMEM(shape, jnp.float32)

    return pl.pallas_call(
        functools.partial(fused_kernel, strips, parts),
        out_shape=(
            jax.ShapeDtypeStruct((2, 8, cols), jnp.float32),
            jax.ShapeDtypeStruct((8, cols), jnp.float32),
        ),
        in_specs=[pl.BlockSpec(memory_space=pl.ANY)] * len(fields),
        out_specs=(pl.BlockSpec(memory_space=pltpu.VMEM),) * 2,
        scratch_shapes=[pltpu.VMEM(x.shape, x.dtype) for x in fields]
        + [
            vmem(strips, 4, slots),
            vmem(strips, 4, slots),
            vmem(total, 8, LANES),
            vmem(parts - 1, span, 8, LANES),
            vmem(3, total, 8, LANES),
            vmem(parts - 1, 3, span, 8, LANES),
            vmem(9 * 8 * (cols // WIN), WIN),
            vmem(strips, 6, 8, WIN),
            vmem(strips, 6, 8, WIN),
            vmem(strips, 8, WIN),
            vmem(strips, 8, WIN),
            vmem(strips, 3, 8, WIN),
            vmem(strips, 3, 8, WIN),
            vmem(10, 8, strips, WIN),
            vmem(2, 2, 8, strips, WIN),
            vmem(2, 9, 8, strips, WIN),
            vmem(2, 8, strips, WIN),
            vmem(2, 8, strips, WIN),
            vmem(strips, 2, 8, LANES),
            vmem(strips, 2, 8, LANES),
            vmem(2, tiles, 8, LANES),
            vmem(strips, 8, LANES),
            vmem(strips, 8, LANES),
            vmem(1, tiles, 8, LANES),
            pltpu.SemaphoreType.DMA((6, strips - 1)),
            pltpu.SemaphoreType.DMA((6, strips - 1)),
            pltpu.SemaphoreType.DMA((4, parts - 1)),
            pltpu.SemaphoreType.DMA((4, parts - 1)),
            pltpu.SemaphoreType.DMA((len(fields),)),
        ],
        compiler_params=pltpu.CompilerParams(
            collective_id=0, has_side_effects=True, vmem_limit_bytes=VMEM_LIMIT
        ),
    )(*fields)


def solution(mesh):
    return jax.shard_map(
        on_device,
        mesh=mesh,
        in_specs=(
            P(None, "tile", None),
            P("layer", "tile", None),
            P("tile", None),
            P("tile", None),
            P("tile", None),
            P("tile", None),
            P(None, "tile", None),
            P("tile", "layer", None, None),
            P("tile", "layer", None, None),
            P("tile", "layer", None, None),
            P("tile", "layer", None, None),
            P("tile", "layer", None),
        ),
        out_specs=(P(None, "tile", None), P("tile", None)),
        check_vma=False,
    )
```

```python
import functools

import jax
import jax.numpy as jnp
from jax import lax
from jax.experimental import pallas as pl
from jax.experimental.pallas import tpu as pltpu
from jax.sharding import PartitionSpec as P

SWEEPS = 40
OMEGA = 0.5
REGULAR = 0.01
HALO = 16
LANES = 128
WIN = LANES
BLOCK = 2 * LANES
OFF = LANES - HALO
VMEM_LIMIT = 60 * 1024 * 1024


def scatter_maps(cell, east, north, weight, acc_ref, cols, first):
    blocks = cols // BLOCK
    slots = cell.shape[1]
    row = jnp.zeros_like(cell)
    for r in range(1, 8):
        row = row + jnp.where(cell >= r * cols, 1, 0)
    rem = cell - row * cols
    high = (rem // BLOCK) * 8 + row
    low = rem % BLOCK
    hit = lax.broadcasted_iota(jnp.int32, (8 * blocks, slots), 0) == high
    terms = []
    for value in (weight, weight * east, weight * north):
        rest = value
        for _ in range(3):
            part = rest.astype(jnp.bfloat16).astype(jnp.float32)
            rest = rest - part
            terms.append(jnp.where(hit, part, 0.0).astype(jnp.bfloat16))
    lhs = jnp.concatenate(terms, axis=0)
    rhs = jnp.where(
        lax.broadcasted_iota(jnp.int32, (BLOCK, slots), 0) == low, 1.0, 0.0
    ).astype(jnp.bfloat16)
    prod = lax.dot_general(
        lhs, rhs, (((1,), (1,)), ((), ())), preferred_element_type=jnp.float32
    )
    if first:
        acc_ref[...] = prod
    else:
        acc_ref[...] += prod


def east_of(x):
    return pltpu.roll(x, WIN - 1, 1)


def west_of(x):
    return pltpu.roll(x, 1, 1)


def up(x):
    return pltpu.roll(x, x.shape[0] - 1, 0)


def down(x):
    return pltpu.roll(x, 1, 0)


def run_sweeps(state, coef, force, count):
    def wide(x):
        return (x, east_of(x), west_of(x))

    def rows(slot, a):
        return (wide(state[slot, 0, a]), wide(state[slot, 1, a]))

    def one(src, dst):
        first = rows(src, 0)
        last_u, last_v = state[src, 0, 7], state[src, 1, 7]
        before = (wide(down(last_u)), wide(down(last_v)))
        here = first
        for a in range(8):
            if a < 7:
                after = rows(src, a + 1)
            else:
                after = (wide(up(state[src, 0, 0])), wide(up(state[src, 1, 0])))
            for f in range(2):
                g = 1 - f
                c = lambda k: coef[f, k, a]
                near = c(0) * here[f][0] + force[f, a]
                near = near + (c(3) * here[f][1] + c(4) * here[f][2])
                over = c(1) * after[f][0] + (c(5) * after[g][1] + c(6) * after[g][2])
                under = c(2) * before[f][0] + (c(7) * before[g][1] + c(8) * before[g][2])
                new = near + (over + under)
                state[dst, f, a] = new
            before, here = here, after

    def two(step, carry):
        one(0, 1)
        one(1, 0)
        return carry

    lax.fori_loop(0, count // 2, two, 0)


def make_coefs(layers, get, state, coef, gain, force):
    strips = state.shape[3]
    index = lax.broadcasted_iota(jnp.int32, (strips, WIN), 0)
    not_top = jnp.where(index == strips - 1, 0.0, 1.0)
    not_low = jnp.where(index == 0, 0.0, 1.0)

    def north(x, a):
        return x[a + 1] if a < 7 else up(x[0]) * not_top

    def south(x, a):
        return x[a - 1] if a > 0 else down(x[7]) * not_low

    u = [get(0, a) for a in range(8)]
    v = [get(1, a) for a in range(8)]
    visc = []
    for a in range(8):
        ux = 0.5 * (north(u, a) - south(u, a))
        vx = 0.5 * (north(v, a) - south(v, a))
        uy = 0.5 * (east_of(u[a]) - west_of(u[a]))
        vy = 0.5 * (east_of(v[a]) - west_of(v[a]))
        shear = uy + vx
        strain = ux * ux + vy * vy + ux * vy + 0.25 * shear * shear + REGULAR
        rate = jnp.exp(jnp.log(strain) * (-1.0 / 3.0))
        visc.append(0.5 * rate * get(6, a) / layers)
        state[0, 0, a] = u[a]
        state[0, 1, a] = v[a]
    for a in range(8):
        here = visc[a]
        vn, vs, ve, vw = north(visc, a), south(visc, a), east_of(here), west_of(here)
        fn, fs, fe, fw = (0.5 * (here + x) for x in (vn, vs, ve, vw))
        drag, inside = get(2, a), get(3, a)
        top = not_top if a == 7 else 1.0
        low = not_low if a == 0 else 1.0
        for f in range(2):
            rg, cg = (4.0, 1.0) if f == 0 else (1.0, 4.0)
            rx, cx = (0.5, 0.25) if f == 0 else (0.25, 0.5)
            spread = rg * (fn + fs) + cg * (fe + fw) + drag
            g = OMEGA * inside / (spread + 1.0 - inside)
            coef[f, 0, a] = inside - g * spread
            coef[f, 1, a] = g * rg * fn * top
            coef[f, 2, a] = g * rg * fs * low
            coef[f, 3, a] = g * cg * fe
            coef[f, 4, a] = g * cg * fw
            coef[f, 5, a] = g * (rx * vn + cx * ve) * top
            coef[f, 6, a] = -g * (rx * vn + cx * vw) * top
            coef[f, 7, a] = -g * (rx * vs + cx * ve) * low
            coef[f, 8, a] = g * (rx * vs + cx * vw) * low
            gain[f, a] = g
            force[f, a] = g * get(4 + f, a)


MESH = pl.DeviceIdType.MESH
LEGS = (14, 14, 12)


def exchange(axis, peers, source, target, send_sem, recv_sem):
    copies = []
    for k, peer in enumerate(peers):
        copy = pltpu.make_async_remote_copy(
            src_ref=source(k, peer),
            dst_ref=target(k),
            send_sem=send_sem.at[k],
            recv_sem=recv_sem.at[k],
            device_id={axis: peer},
            device_id_type=MESH,
        )
        copy.start()
        copies.append(copy)
    return copies


def finish(copies):
    for copy in copies:
        copy.wait()


def cut_window(tiles, own, pos):
    at = OFF + own * pos
    first, skip = at // LANES, at % LANES
    if skip == 0:
        return tiles[first]
    keep = lax.broadcasted_iota(jnp.int32, (8, LANES), 1) < LANES - skip
    turned = [pltpu.roll(tiles[first + j], LANES - skip, 1) for j in range(2)]
    return jnp.where(keep, turned[0], turned[1])


def snake(index, strips):
    inner = max(1, strips // 4)
    outer, rest = index // inner, index % inner
    return outer * inner + rest + (outer % 2) * (inner - 1 - 2 * rest)


def position(tile, layer, strips):
    pos = snake(tile, strips)
    return pos + (layer % 2) * (strips - 1 - 2 * pos)


def device_at(place, strips, parts):
    place = place % (strips * parts)
    layer, pos = place // strips, place % strips
    return snake(pos + (layer % 2) * (strips - 1 - 2 * pos), strips), layer


def join_pieces(pieces, own, q):
    lane = lax.broadcasted_iota(jnp.int32, (8, LANES), 1)
    tile = None
    for s, piece in enumerate(pieces):
        shift = own * s - LANES * q
        if shift + own <= 0 or shift >= LANES:
            continue
        moved = piece if shift % LANES == 0 else pltpu.roll(piece, shift % LANES, 1)
        tile = moved if tile is None else jnp.where(lane >= shift, moved, tile)
    return tile


def fused_kernel(
    strips,
    parts,
    *refs,
):
    args, (vel_ref, grad_ref), held = refs[:12], refs[12:14], refs[14:26]
    (
    obs_out,
    obs_in,
    hard_buf,
    hard_in,
    maps_buf,
    maps_in,
    acc_ref,
    send_a,
    recv_a,
    send_b,
    recv_b,
    send_c,
    recv_c,
    x_ref,
    state,
    coef,
    gain,
    force,
    vel_out,
    vel_in,
    vel_all,
    grad_out,
    grad_in,
    grad_all,
    tile_send,
    tile_recv,
    layer_send,
    layer_recv,
    load_sem,
    halo_out,
    halo_in,
    halo_send,
    halo_recv,
    ) = refs[26:]
    (
        guess_ref,
        hard_ref,
        thick_ref,
        fric_ref,
        ground_ref,
        mask_ref,
        drive_ref,
        cell_ref,
        east_ref,
        north_ref,
        weight_ref,
        count_ref,
    ) = held
    cols = thick_ref.shape[1]
    group = cols // parts
    own = group // strips
    step = group // LANES
    span = hard_in.shape[1]
    layers = float(hard_ref.shape[0] * parts)
    me, layer = lax.axis_index("tile"), lax.axis_index("layer")
    others = [lax.rem(me + k, strips) for k in range(1, strips)]
    mates = [lax.rem(layer + k, parts) for k in range(1, parts)]

    spot = position(me, layer, strips)
    place = layer * strips + spot
    sides = [device_at(place + strips * parts - 1, strips, parts), device_at(place + 1, strips, parts)]

    barrier = pltpu.get_barrier_semaphore()
    for peer in others:
        pl.semaphore_signal(barrier, inc=1, device_id={"tile": peer}, device_id_type=MESH)
    for peer in mates:
        pl.semaphore_signal(barrier, inc=1, device_id={"layer": peer}, device_id_type=MESH)

    arrivals = [
        pltpu.make_async_copy(args[n], held[n], load_sem.at[n]) for n in range(len(args))
    ]
    for n in (7, 8, 9, 10, 11, 1, 2, 0, 3, 4, 5, 6):
        arrivals[n].start()

    for n in (1, 2):
        arrivals[n].wait()
    zero = jnp.zeros((8, LANES), jnp.float32)
    total = hard_buf.shape[0]
    for i in range(total):
        at = (i - 1) * LANES
        if 0 <= at < cols:
            value = hard_ref[0, :, at : at + LANES]
            for k in range(1, hard_ref.shape[0]):
                value = value + hard_ref[k, :, at : at + LANES]
            hard_buf[i] = value * thick_ref[:, at : at + LANES]
        else:
            hard_buf[i] = zero
            for f in range(3):
                maps_buf[f, i] = zero
    for n in (7, 8, 9, 10, 11):
        arrivals[n].wait()
    slot = lax.broadcasted_iota(jnp.int32, (1, cell_ref.shape[3]), 1)
    for d in range(strips):
        obs_out[d, 0:1] = cell_ref[0, 0, d : d + 1].astype(jnp.float32)
        obs_out[d, 1:2] = east_ref[0, 0, d : d + 1]
        obs_out[d, 2:3] = north_ref[0, 0, d : d + 1]
        obs_out[d, 3:4] = jnp.where(slot < count_ref[0, :, d : d + 1], weight_ref[0, 0, d : d + 1], 0.0)

    for n in (0, 3, 4, 5, 6):
        arrivals[n].wait()
    def group_tiles(load):
        tiles = []
        for i in range(span):
            at = group * layer + (i - 1) * LANES
            if 1 <= i <= step:
                tiles.append(load(pl.ds(pl.multiple_of(at, LANES), LANES)))
            else:
                inside = jnp.logical_and(at >= 0, at < cols)
                safe = jnp.where(inside, at, 0)
                value = load(pl.ds(pl.multiple_of(safe, LANES), LANES))
                tiles.append(jnp.where(inside, value, 0.0))
        return tiles

    loads = [
        lambda at: guess_ref[0, :, at],
        lambda at: guess_ref[1, :, at],
        lambda at: fric_ref[:, at] * ground_ref[:, at].astype(jnp.float32),
        lambda at: mask_ref[:, at].astype(jnp.float32),
        lambda at: drive_ref[0, :, at],
        lambda at: drive_ref[1, :, at],
    ]
    for f, load in enumerate(loads):
        tiles = group_tiles(load)
        for t in range(strips):
            send_a[t, f] = cut_window(tiles, own, t)

    def tile_exchange(n, out, into, back=False, window=False):
        return exchange(
            "tile",
            others,
            lambda k, peer: out.at[position(peer, layer, strips) if window else peer],
            lambda k: into.at[spot if back else me],
            tile_send.at[n],
            tile_recv.at[n],
        )

    pl.semaphore_wait(barrier, strips + parts - 2)
    hard_copies = exchange(
        "layer",
        mates,
        lambda k, peer: hard_buf.at[pl.ds(step * peer, span)],
        lambda k: hard_in.at[k],
        layer_send.at[0],
        layer_recv.at[0],
    )
    obs_copies = tile_exchange(0, obs_out, obs_in)
    a_copies = tile_exchange(1, send_a, recv_a, window=True)
    obs_in[me] = obs_out[me]
    recv_a[me] = send_a[spot]

    finish(hard_copies)
    tiles = []
    for i in range(span):
        value = hard_buf[step * layer + i]
        for k in range(parts - 1):
            value = value + hard_in[k, i]
        tiles.append(value)
    for t in range(strips):
        send_b[t] = cut_window(tiles, own, t)
    b_copies = tile_exchange(2, send_b, recv_b, window=True)
    recv_b[me] = send_b[spot]

    finish(obs_copies)
    for s in range(strips):
        scatter_maps(
            obs_in[s, 0:1].astype(jnp.int32),
            obs_in[s, 1:2],
            obs_in[s, 2:3],
            obs_in[s, 3:4],
            acc_ref,
            cols,
            s == 0,
        )
    n = 8 * (cols // BLOCK)
    for f in range(3):
        for i in range(cols // LANES):
            at = 3 * f * n + 8 * (i // 2)
            half = slice((i % 2) * LANES, (i % 2 + 1) * LANES)
            maps_buf[f, i + 1] = (
                acc_ref[at : at + 8, half]
                + acc_ref[at + n : at + n + 8, half]
                + acc_ref[at + 2 * n : at + 2 * n + 8, half]
            )
    maps_copies = exchange(
        "layer",
        mates,
        lambda k, peer: maps_buf.at[:, pl.ds(step * peer, span)],
        lambda k: maps_in.at[k],
        layer_send.at[1],
        layer_recv.at[1],
    )

    finish(a_copies)
    finish(b_copies)
    for f in range(6):
        x_ref[f] = jnp.swapaxes(recv_a[:, f], 0, 1)
    x_ref[6] = jnp.swapaxes(recv_b[...], 0, 1)

    def get(f, a):
        return x_ref[f, a]

    make_coefs(layers, get, state, coef, gain, force)
    lane = lax.broadcasted_iota(jnp.int32, (strips, LANES), 1)

    def send_halos(n):
        for f in range(2):
            left = right = None
            for a in range(8):
                value = state[0, f, a]
                to_left = pltpu.roll(value, (HALO * a - HALO) % LANES, 1)
                to_right = pltpu.roll(value, (HALO * a - own) % LANES, 1)
                left = to_left if a == 0 else jnp.where(lane >= HALO * a, to_left, left)
                right = to_right if a == 0 else jnp.where(lane >= HALO * a, to_right, right)
            halo_out[n, 0, f] = left
            halo_out[n, 1, f] = right
        copies = []
        for side, (tile, part) in enumerate(sides):
            copy = pltpu.make_async_remote_copy(
                src_ref=halo_out.at[n, side],
                dst_ref=halo_in.at[n, side],
                send_sem=halo_send.at[n, side],
                recv_sem=halo_recv.at[n, side],
                device_id={"tile": tile, "layer": part},
                device_id_type=MESH,
            )
            copy.start()
            copies.append(copy)
        return copies

    def take_halos(n, copies):
        finish(copies)
        low = lane < HALO
        high = jnp.logical_and(lane >= HALO + own, lane < 2 * HALO + own)
        for f in range(2):
            from_left = jnp.where(place > 0, halo_in[n, 1, f], 0.0)
            from_right = jnp.where(place < strips * parts - 1, halo_in[n, 0, f], 0.0)
            for a in range(8):
                west = pltpu.roll(from_left, (LANES - HALO * a) % LANES, 1)
                east = pltpu.roll(from_right, (HALO + own - HALO * a) % LANES, 1)
                value = jnp.where(low, west, state[0, f, a])
                state[0, f, a] = jnp.where(high, east, value)

    run_sweeps(state, coef, force, LEGS[0])
    halos = send_halos(0)
    finish(maps_copies)
    for f in range(3):
        tiles = []
        for i in range(span):
            value = maps_buf[f, step * layer + i]
            for k in range(parts - 1):
                value = value + maps_in[k, f, i]
            tiles.append(value)
        for t in range(strips):
            send_c[t, f] = cut_window(tiles, own, t)
    c_copies = tile_exchange(3, send_c, recv_c, window=True)
    recv_c[me] = send_c[spot]
    take_halos(0, halos)
    run_sweeps(state, coef, force, LEGS[1])
    take_halos(1, send_halos(1))
    run_sweeps(state, coef, force, LEGS[2])
    halos = send_halos(2)

    def own_part(value):
        return pltpu.roll(value, WIN - HALO, 1)

    for f in range(2):
        parts_f = jnp.stack([own_part(state[0, f, a]) for a in range(8)], 0)
        vel_out[:, f] = jnp.swapaxes(parts_f, 0, 1)
    vel_copies = tile_exchange(4, vel_out, vel_in, back=True)
    vel_in[spot] = vel_out[me]
    finish(c_copies)
    for f in range(3):
        x_ref[7 + f] = jnp.swapaxes(recv_c[:, f], 0, 1)
    take_halos(2, halos)
    for a in range(8):
        for f in range(2):
            vel = state[0, f, a]
            force[f, a] = gain[f, a] * (vel * get(7, a) - get(8 + f, a))
            gain[f, a] = vel
            state[0, f, a] = jnp.zeros_like(vel)
    run_sweeps(state, coef, force, LEGS[0])

    def layer_gather(n, every):
        here = every.at[:, pl.ds(step * layer, step)]
        return exchange(
            "layer", mates, lambda k, peer: here, lambda k: here, layer_send.at[n], layer_recv.at[n]
        )

    halos = send_halos(3)
    finish(vel_copies)
    for f in range(2):
        pieces = [vel_in[s, f] for s in range(strips)]
        for q in range(step):
            vel_all[f, step * layer + q] = join_pieces(pieces, own, q)
    gather_copies = layer_gather(2, vel_all)
    take_halos(3, halos)
    run_sweeps(state, coef, force, LEGS[1])
    take_halos(4, send_halos(4))
    run_sweeps(state, coef, force, LEGS[2])

    rows = jnp.stack(
        [
            own_part(
                -(get(2, a) * (gain[0, a] * state[0, 0, a] + gain[1, a] * state[0, 1, a]))
            )
            for a in range(8)
        ],
        0,
    )
    grad_out[...] = jnp.swapaxes(rows, 0, 1)
    grad_copies = tile_exchange(5, grad_out, grad_in, back=True)
    grad_in[spot] = grad_out[me]
    finish(gather_copies)
    for f in range(2):
        for i in range(cols // LANES):
            vel_ref[f, :, i * LANES : (i + 1) * LANES] = vel_all[f, i]
    finish(grad_copies)
    pieces = [grad_in[s] for s in range(strips)]
    for q in range(step):
        grad_all[0, step * layer + q] = join_pieces(pieces, own, q)
    finish(layer_gather(3, grad_all))
    for i in range(cols // LANES):
        grad_ref[:, i * LANES : (i + 1) * LANES] = grad_all[0, i]


def on_device(*fields):
    strips, parts = lax.axis_size("tile"), lax.axis_size("layer")
    cols = fields[2].shape[1]
    slots = fields[7].shape[3]
    group = cols // parts
    own = group // strips
    span = -(-(OFF + own * (strips - 1) + WIN) // LANES)
    total = group // LANES * (parts - 1) + span
    tiles = cols // LANES

    def vmem(*shape):
        return pltpu.VMEM(shape, jnp.float32)

    return pl.pallas_call(
        functools.partial(fused_kernel, strips, parts),
        out_shape=(
            jax.ShapeDtypeStruct((2, 8, cols), jnp.float32),
            jax.ShapeDtypeStruct((8, cols), jnp.float32),
        ),
        in_specs=[pl.BlockSpec(memory_space=pl.ANY)] * len(fields),
        out_specs=(pl.BlockSpec(memory_space=pltpu.VMEM),) * 2,
        scratch_shapes=[pltpu.VMEM(x.shape, x.dtype) for x in fields]
        + [
            vmem(strips, 4, slots),
            vmem(strips, 4, slots),
            vmem(total, 8, LANES),
            vmem(parts - 1, span, 8, LANES),
            vmem(3, total, 8, LANES),
            vmem(parts - 1, 3, span, 8, LANES),
            vmem(9 * 8 * (cols // BLOCK), BLOCK),
            vmem(strips, 6, 8, WIN),
            vmem(strips, 6, 8, WIN),
            vmem(strips, 8, WIN),
            vmem(strips, 8, WIN),
            vmem(strips, 3, 8, WIN),
            vmem(strips, 3, 8, WIN),
            vmem(10, 8, strips, WIN),
            vmem(2, 2, 8, strips, WIN),
            vmem(2, 9, 8, strips, WIN),
            vmem(2, 8, strips, WIN),
            vmem(2, 8, strips, WIN),
            vmem(strips, 2, 8, LANES),
            vmem(strips, 2, 8, LANES),
            vmem(2, tiles, 8, LANES),
            vmem(strips, 8, LANES),
            vmem(strips, 8, LANES),
            vmem(1, tiles, 8, LANES),
            pltpu.SemaphoreType.DMA((6, strips - 1)),
            pltpu.SemaphoreType.DMA((6, strips - 1)),
            pltpu.SemaphoreType.DMA((4, parts - 1)),
            pltpu.SemaphoreType.DMA((4, parts - 1)),
            pltpu.SemaphoreType.DMA((len(fields),)),
            vmem(5, 2, 2, strips, LANES),
            vmem(5, 2, 2, strips, LANES),
            pltpu.SemaphoreType.DMA((5, 2)),
            pltpu.SemaphoreType.DMA((5, 2)),
        ],
        compiler_params=pltpu.CompilerParams(
            collective_id=0, has_side_effects=True, vmem_limit_bytes=VMEM_LIMIT
        ),
    )(*fields)


def solution(mesh):
    return jax.shard_map(
        on_device,
        mesh=mesh,
        in_specs=(
            P(None, "tile", None),
            P("layer", "tile", None),
            P("tile", None),
            P("tile", None),
            P("tile", None),
            P("tile", None),
            P(None, "tile", None),
            P("tile", "layer", None, None),
            P("tile", "layer", None, None),
            P("tile", "layer", None, None),
            P("tile", "layer", None, None),
            P("tile", "layer", None),
        ),
        out_specs=(P(None, "tile", None), P("tile", None)),
        check_vma=False,
    )
```

```python
import functools

import jax
import jax.numpy as jnp
from jax import lax
from jax.experimental import pallas as pl
from jax.experimental.pallas import tpu as pltpu
from jax.sharding import PartitionSpec as P

SWEEPS = 40
OMEGA = 0.5
REGULAR = 0.01
HALO = 2 * SWEEPS
WIN = 256
LANES = 128
OFF = LANES - HALO
VMEM_LIMIT = 60 * 1024 * 1024


def scatter_maps(cell, east, north, weight, acc_ref, cols, first):
    blocks = cols // WIN
    slots = cell.shape[1]
    row = jnp.zeros_like(cell)
    for r in range(1, 8):
        row = row + jnp.where(cell >= r * cols, 1, 0)
    rem = cell - row * cols
    high = (rem // WIN) * 8 + row
    low = rem % WIN
    hit = lax.broadcasted_iota(jnp.int32, (8 * blocks, slots), 0) == high
    terms = []
    for value in (weight, weight * east, weight * north):
        rest = value
        for _ in range(3):
            part = rest.astype(jnp.bfloat16).astype(jnp.float32)
            rest = rest - part
            terms.append(jnp.where(hit, part, 0.0).astype(jnp.bfloat16))
    lhs = jnp.concatenate(terms, axis=0)
    rhs = jnp.where(
        lax.broadcasted_iota(jnp.int32, (WIN, slots), 0) == low, 1.0, 0.0
    ).astype(jnp.bfloat16)
    prod = lax.dot_general(
        lhs, rhs, (((1,), (1,)), ((), ())), preferred_element_type=jnp.float32
    )
    if first:
        acc_ref[...] = prod
    else:
        acc_ref[...] += prod


def split_columns(x):
    source = lax.broadcasted_iota(jnp.int32, (WIN, WIN), 0)
    target = lax.broadcasted_iota(jnp.int32, (WIN, WIN), 1)
    wanted = jnp.where(target < LANES, 2 * target, 2 * target - WIN + 1)
    pick = jnp.where(source == wanted, 1.0, 0.0)
    return jnp.dot(
        x, pick, precision=lax.Precision.HIGHEST, preferred_element_type=jnp.float32
    )


def own_columns(x):
    source = lax.broadcasted_iota(jnp.int32, (WIN, LANES), 0)
    target = lax.broadcasted_iota(jnp.int32, (WIN, LANES), 1)
    column = jnp.where(source < LANES, 2 * source, 2 * source - WIN + 1)
    pick = jnp.where(column == target + HALO, 1.0, 0.0)
    return jnp.dot(
        x, pick, precision=lax.Precision.HIGHEST, preferred_element_type=jnp.float32
    )


def east_of(x):
    even, odd = x[:, :LANES], x[:, LANES:]
    return jnp.concatenate([odd, pltpu.roll(even, LANES - 1, 1)], axis=1)


def west_of(x):
    even, odd = x[:, :LANES], x[:, LANES:]
    return jnp.concatenate([pltpu.roll(odd, 1, 1), even], axis=1)


def up(x):
    return pltpu.roll(x, x.shape[0] - 1, 0)


def down(x):
    return pltpu.roll(x, 1, 0)


def run_sweeps(state, coef, force, count):
    def wide(x):
        return (x, east_of(x), west_of(x))

    def rows(slot, a):
        return (wide(state[slot, 0, a]), wide(state[slot, 1, a]))

    def one(src, dst):
        first = rows(src, 0)
        last_u, last_v = state[src, 0, 7], state[src, 1, 7]
        before = (wide(down(last_u)), wide(down(last_v)))
        here = first
        for a in range(8):
            if a < 7:
                after = rows(src, a + 1)
            else:
                after = (wide(up(state[src, 0, 0])), wide(up(state[src, 1, 0])))
            for f in range(2):
                g = 1 - f
                c = lambda k: coef[f, k, a]
                near = c(0) * here[f][0] + force[f, a]
                near = near + (c(3) * here[f][1] + c(4) * here[f][2])
                over = c(1) * after[f][0] + (c(5) * after[g][1] + c(6) * after[g][2])
                under = c(2) * before[f][0] + (c(7) * before[g][1] + c(8) * before[g][2])
                new = near + (over + under)
                state[dst, f, a] = new
            before, here = here, after

    def two(step, carry):
        one(0, 1)
        one(1, 0)
        return carry

    lax.fori_loop(0, count // 2, two, 0)


def make_coefs(layers, get, state, coef, gain, force):
    strips = state.shape[3]
    index = lax.broadcasted_iota(jnp.int32, (strips, WIN), 0)
    not_top = jnp.where(index == strips - 1, 0.0, 1.0)
    not_low = jnp.where(index == 0, 0.0, 1.0)

    def north(x, a):
        return x[a + 1] if a < 7 else up(x[0]) * not_top

    def south(x, a):
        return x[a - 1] if a > 0 else down(x[7]) * not_low

    u = [get(0, a) for a in range(8)]
    v = [get(1, a) for a in range(8)]
    visc = []
    for a in range(8):
        ux = 0.5 * (north(u, a) - south(u, a))
        vx = 0.5 * (north(v, a) - south(v, a))
        uy = 0.5 * (east_of(u[a]) - west_of(u[a]))
        vy = 0.5 * (east_of(v[a]) - west_of(v[a]))
        shear = uy + vx
        strain = ux * ux + vy * vy + ux * vy + 0.25 * shear * shear + REGULAR
        rate = jnp.exp(jnp.log(strain) * (-1.0 / 3.0))
        visc.append(0.5 * rate * get(6, a) / layers)
        state[0, 0, a] = u[a]
        state[0, 1, a] = v[a]
    for a in range(8):
        here = visc[a]
        vn, vs, ve, vw = north(visc, a), south(visc, a), east_of(here), west_of(here)
        fn, fs, fe, fw = (0.5 * (here + x) for x in (vn, vs, ve, vw))
        drag, inside = get(2, a), get(3, a)
        top = not_top if a == 7 else 1.0
        low = not_low if a == 0 else 1.0
        for f in range(2):
            rg, cg = (4.0, 1.0) if f == 0 else (1.0, 4.0)
            rx, cx = (0.5, 0.25) if f == 0 else (0.25, 0.5)
            spread = rg * (fn + fs) + cg * (fe + fw) + drag
            g = OMEGA * inside / (spread + 1.0 - inside)
            coef[f, 0, a] = inside - g * spread
            coef[f, 1, a] = g * rg * fn * top
            coef[f, 2, a] = g * rg * fs * low
            coef[f, 3, a] = g * cg * fe
            coef[f, 4, a] = g * cg * fw
            coef[f, 5, a] = g * (rx * vn + cx * ve) * top
            coef[f, 6, a] = -g * (rx * vn + cx * vw) * top
            coef[f, 7, a] = -g * (rx * vs + cx * ve) * low
            coef[f, 8, a] = g * (rx * vs + cx * vw) * low
            gain[f, a] = g
            force[f, a] = g * get(4 + f, a)


MESH = pl.DeviceIdType.MESH
EARLY = 4
RETURN = 16


def exchange(axis, peers, source, target, send_sem, recv_sem):
    copies = []
    for k, peer in enumerate(peers):
        copy = pltpu.make_async_remote_copy(
            src_ref=source(k, peer),
            dst_ref=target(k),
            send_sem=send_sem.at[k],
            recv_sem=recv_sem.at[k],
            device_id={axis: peer},
            device_id_type=MESH,
        )
        copy.start()
        copies.append(copy)
    return copies


def finish(copies):
    for copy in copies:
        copy.wait()


def cut_window(tiles, own, t):
    at = OFF + own * t
    first, skip = at // LANES, at % LANES
    if skip == 0:
        return jnp.concatenate([tiles[first], tiles[first + 1]], axis=1)
    keep = lax.broadcasted_iota(jnp.int32, (8, LANES), 1) < LANES - skip
    turned = [pltpu.roll(tiles[first + j], LANES - skip, 1) for j in range(3)]
    return jnp.concatenate(
        [jnp.where(keep, turned[j], turned[j + 1]) for j in range(2)], axis=1
    )


def join_pieces(pieces, own, q):
    lane = lax.broadcasted_iota(jnp.int32, (8, LANES), 1)
    tile = None
    for s, piece in enumerate(pieces):
        shift = own * s - LANES * q
        if shift + own <= 0 or shift >= LANES:
            continue
        moved = piece if shift % LANES == 0 else pltpu.roll(piece, shift % LANES, 1)
        tile = moved if tile is None else jnp.where(lane >= shift, moved, tile)
    return tile


def fused_kernel(
    strips,
    parts,
    *refs,
):
    args, (vel_ref, grad_ref), held = refs[:12], refs[12:14], refs[14:26]
    (
    obs_out,
    obs_in,
    hard_buf,
    hard_in,
    maps_buf,
    maps_in,
    acc_ref,
    send_a,
    recv_a,
    send_b,
    recv_b,
    send_c,
    recv_c,
    x_ref,
    state,
    coef,
    gain,
    force,
    vel_out,
    vel_in,
    vel_all,
    grad_out,
    grad_in,
    grad_all,
    tile_send,
    tile_recv,
    layer_send,
    layer_recv,
    load_sem,
    ) = refs[26:]
    (
        guess_ref,
        hard_ref,
        thick_ref,
        fric_ref,
        ground_ref,
        mask_ref,
        drive_ref,
        cell_ref,
        east_ref,
        north_ref,
        weight_ref,
        count_ref,
    ) = held
    cols = thick_ref.shape[1]
    group = cols // parts
    own = group // strips
    step = group // LANES
    span = hard_in.shape[1]
    layers = float(hard_ref.shape[0] * parts)
    me, layer = lax.axis_index("tile"), lax.axis_index("layer")
    others = [lax.rem(me + k, strips) for k in range(1, strips)]
    mates = [lax.rem(layer + k, parts) for k in range(1, parts)]

    barrier = pltpu.get_barrier_semaphore()
    for peer in others:
        pl.semaphore_signal(barrier, inc=1, device_id={"tile": peer}, device_id_type=MESH)
    for peer in mates:
        pl.semaphore_signal(barrier, inc=1, device_id={"layer": peer}, device_id_type=MESH)

    arrivals = [
        pltpu.make_async_copy(args[n], held[n], load_sem.at[n]) for n in range(len(args))
    ]
    for n in (7, 8, 9, 10, 11, 1, 2, 0, 3, 4, 5, 6):
        arrivals[n].start()

    for n in (1, 2):
        arrivals[n].wait()
    zero = jnp.zeros((8, LANES), jnp.float32)
    total = hard_buf.shape[0]
    for i in range(total):
        at = (i - 1) * LANES
        if 0 <= at < cols:
            value = hard_ref[0, :, at : at + LANES]
            for k in range(1, hard_ref.shape[0]):
                value = value + hard_ref[k, :, at : at + LANES]
            hard_buf[i] = value * thick_ref[:, at : at + LANES]
        else:
            hard_buf[i] = zero
            for f in range(3):
                maps_buf[f, i] = zero
    for n in (7, 8, 9, 10, 11):
        arrivals[n].wait()
    slot = lax.broadcasted_iota(jnp.int32, (1, cell_ref.shape[3]), 1)
    for d in range(strips):
        obs_out[d, 0:1] = cell_ref[0, 0, d : d + 1].astype(jnp.float32)
        obs_out[d, 1:2] = east_ref[0, 0, d : d + 1]
        obs_out[d, 2:3] = north_ref[0, 0, d : d + 1]
        obs_out[d, 3:4] = jnp.where(slot < count_ref[0, :, d : d + 1], weight_ref[0, 0, d : d + 1], 0.0)

    for n in (0, 3, 4, 5, 6):
        arrivals[n].wait()
    def group_tiles(load):
        tiles = []
        for i in range(span):
            at = group * layer + (i - 1) * LANES
            if 1 <= i <= step:
                tiles.append(load(pl.ds(pl.multiple_of(at, LANES), LANES)))
            else:
                inside = jnp.logical_and(at >= 0, at < cols)
                safe = jnp.where(inside, at, 0)
                value = load(pl.ds(pl.multiple_of(safe, LANES), LANES))
                tiles.append(jnp.where(inside, value, 0.0))
        return tiles

    loads = [
        lambda at: guess_ref[0, :, at],
        lambda at: guess_ref[1, :, at],
        lambda at: fric_ref[:, at] * ground_ref[:, at].astype(jnp.float32),
        lambda at: mask_ref[:, at].astype(jnp.float32),
        lambda at: drive_ref[0, :, at],
        lambda at: drive_ref[1, :, at],
    ]
    for f, load in enumerate(loads):
        tiles = group_tiles(load)
        for t in range(strips):
            send_a[t, f] = cut_window(tiles, own, t)

    def split_all(ref):
        rows = ref[...].reshape(-1, WIN)
        ref[...] = split_columns(rows).reshape(ref.shape)

    split_all(send_a)

    def tile_exchange(n, out, into):
        return exchange(
            "tile",
            others,
            lambda k, peer: out.at[peer],
            lambda k: into.at[me],
            tile_send.at[n],
            tile_recv.at[n],
        )

    pl.semaphore_wait(barrier, strips + parts - 2)
    hard_copies = exchange(
        "layer",
        mates,
        lambda k, peer: hard_buf.at[pl.ds(step * peer, span)],
        lambda k: hard_in.at[k],
        layer_send.at[0],
        layer_recv.at[0],
    )
    obs_copies = tile_exchange(0, obs_out, obs_in)
    a_copies = tile_exchange(1, send_a, recv_a)
    obs_in[me] = obs_out[me]
    recv_a[me] = send_a[me]

    finish(hard_copies)
    tiles = []
    for i in range(span):
        value = hard_buf[step * layer + i]
        for k in range(parts - 1):
            value = value + hard_in[k, i]
        tiles.append(value)
    for t in range(strips):
        send_b[t] = cut_window(tiles, own, t)
    split_all(send_b)
    b_copies = tile_exchange(2, send_b, recv_b)
    recv_b[me] = send_b[me]

    finish(obs_copies)
    for s in range(strips):
        scatter_maps(
            obs_in[s, 0:1].astype(jnp.int32),
            obs_in[s, 1:2],
            obs_in[s, 2:3],
            obs_in[s, 3:4],
            acc_ref,
            cols,
            s == 0,
        )
    n = 8 * (cols // WIN)
    for f in range(3):
        for i in range(cols // LANES):
            at = 3 * f * n + 8 * (i // 2)
            half = slice((i % 2) * LANES, (i % 2 + 1) * LANES)
            maps_buf[f, i + 1] = (
                acc_ref[at : at + 8, half]
                + acc_ref[at + n : at + n + 8, half]
                + acc_ref[at + 2 * n : at + 2 * n + 8, half]
            )
    maps_copies = exchange(
        "layer",
        mates,
        lambda k, peer: maps_buf.at[:, pl.ds(step * peer, span)],
        lambda k: maps_in.at[k],
        layer_send.at[1],
        layer_recv.at[1],
    )

    finish(a_copies)
    finish(b_copies)
    for f in range(6):
        x_ref[f] = jnp.swapaxes(recv_a[:, f], 0, 1)
    x_ref[6] = jnp.swapaxes(recv_b[...], 0, 1)

    def get(f, a):
        return x_ref[f, a]

    make_coefs(layers, get, state, coef, gain, force)
    run_sweeps(state, coef, force, EARLY)

    finish(maps_copies)
    for f in range(3):
        tiles = []
        for i in range(span):
            value = maps_buf[f, step * layer + i]
            for k in range(parts - 1):
                value = value + maps_in[k, f, i]
            tiles.append(value)
        for t in range(strips):
            send_c[t, f] = cut_window(tiles, own, t)
    split_all(send_c)
    c_copies = tile_exchange(3, send_c, recv_c)
    recv_c[me] = send_c[me]
    run_sweeps(state, coef, force, SWEEPS - EARLY)

    def own_rows(rows):
        picked = own_columns(jnp.concatenate(rows, axis=0))
        return jnp.swapaxes(picked.reshape(8, strips, LANES), 0, 1)

    for f in range(2):
        vel_out[:, f] = own_rows([state[0, f, a] for a in range(8)])
    vel_copies = tile_exchange(4, vel_out, vel_in)
    vel_in[me] = vel_out[me]

    finish(c_copies)
    for f in range(3):
        x_ref[7 + f] = jnp.swapaxes(recv_c[:, f], 0, 1)
    for a in range(8):
        for f in range(2):
            vel = state[0, f, a]
            force[f, a] = gain[f, a] * (vel * get(7, a) - get(8 + f, a))
            gain[f, a] = vel
            state[0, f, a] = jnp.zeros_like(vel)
    run_sweeps(state, coef, force, RETURN)

    def layer_gather(n, every):
        here = every.at[:, pl.ds(step * layer, step)]
        return exchange(
            "layer", mates, lambda k, peer: here, lambda k: here, layer_send.at[n], layer_recv.at[n]
        )

    finish(vel_copies)
    for f in range(2):
        pieces = [vel_in[s, f] for s in range(strips)]
        for q in range(step):
            vel_all[f, step * layer + q] = join_pieces(pieces, own, q)
    gather_copies = layer_gather(2, vel_all)
    run_sweeps(state, coef, force, SWEEPS - RETURN)

    grad_out[...] = own_rows(
        [
            -(get(2, a) * (gain[0, a] * state[0, 0, a] + gain[1, a] * state[0, 1, a]))
            for a in range(8)
        ]
    )
    grad_copies = tile_exchange(5, grad_out, grad_in)
    grad_in[me] = grad_out[me]
    finish(gather_copies)
    for f in range(2):
        for i in range(cols // LANES):
            vel_ref[f, :, i * LANES : (i + 1) * LANES] = vel_all[f, i]
    finish(grad_copies)
    pieces = [grad_in[s] for s in range(strips)]
    for q in range(step):
        grad_all[0, step * layer + q] = join_pieces(pieces, own, q)
    finish(layer_gather(3, grad_all))
    for i in range(cols // LANES):
        grad_ref[:, i * LANES : (i + 1) * LANES] = grad_all[0, i]


def on_device(*fields):
    strips, parts = lax.axis_size("tile"), lax.axis_size("layer")
    cols = fields[2].shape[1]
    slots = fields[7].shape[3]
    group = cols // parts
    own = group // strips
    span = -(-(OFF + own * (strips - 1) + WIN) // LANES)
    total = group // LANES * (parts - 1) + span
    tiles = cols // LANES

    def vmem(*shape):
        return pltpu.VMEM(shape, jnp.float32)

    return pl.pallas_call(
        functools.partial(fused_kernel, strips, parts),
        out_shape=(
            jax.ShapeDtypeStruct((2, 8, cols), jnp.float32),
            jax.ShapeDtypeStruct((8, cols), jnp.float32),
        ),
        in_specs=[pl.BlockSpec(memory_space=pl.ANY)] * len(fields),
        out_specs=(pl.BlockSpec(memory_space=pltpu.VMEM),) * 2,
        scratch_shapes=[pltpu.VMEM(x.shape, x.dtype) for x in fields]
        + [
            vmem(strips, 4, slots),
            vmem(strips, 4, slots),
            vmem(total, 8, LANES),
            vmem(parts - 1, span, 8, LANES),
            vmem(3, total, 8, LANES),
            vmem(parts - 1, 3, span, 8, LANES),
            vmem(9 * 8 * (cols // WIN), WIN),
            vmem(strips, 6, 8, WIN),
            vmem(strips, 6, 8, WIN),
            vmem(strips, 8, WIN),
            vmem(strips, 8, WIN),
            vmem(strips, 3, 8, WIN),
            vmem(strips, 3, 8, WIN),
            vmem(10, 8, strips, WIN),
            vmem(2, 2, 8, strips, WIN),
            vmem(2, 9, 8, strips, WIN),
            vmem(2, 8, strips, WIN),
            vmem(2, 8, strips, WIN),
            vmem(strips, 2, 8, LANES),
            vmem(strips, 2, 8, LANES),
            vmem(2, tiles, 8, LANES),
            vmem(strips, 8, LANES),
            vmem(strips, 8, LANES),
            vmem(1, tiles, 8, LANES),
            pltpu.SemaphoreType.DMA((6, strips - 1)),
            pltpu.SemaphoreType.DMA((6, strips - 1)),
            pltpu.SemaphoreType.DMA((4, parts - 1)),
            pltpu.SemaphoreType.DMA((4, parts - 1)),
            pltpu.SemaphoreType.DMA((len(fields),)),
        ],
        compiler_params=pltpu.CompilerParams(
            collective_id=0, has_side_effects=True, vmem_limit_bytes=VMEM_LIMIT
        ),
    )(*fields)


def solution(mesh):
    return jax.shard_map(
        on_device,
        mesh=mesh,
        in_specs=(
            P(None, "tile", None),
            P("layer", "tile", None),
            P("tile", None),
            P("tile", None),
            P("tile", None),
            P("tile", None),
            P(None, "tile", None),
            P("tile", "layer", None, None),
            P("tile", "layer", None, None),
            P("tile", "layer", None, None),
            P("tile", "layer", None, None),
            P("tile", "layer", None),
        ),
        out_specs=(P(None, "tile", None), P("tile", None)),
        check_vma=False,
    )
```

```python
import functools

import jax
import jax.numpy as jnp
from jax import lax
from jax.experimental import pallas as pl
from jax.experimental.pallas import tpu as pltpu
from jax.sharding import PartitionSpec as P

SWEEPS = 40
OMEGA = 0.5
REGULAR = 0.01
HALO = 2 * SWEEPS
WIN = 256
LANES = 128
OFF = LANES - HALO
VMEM_LIMIT = 60 * 1024 * 1024


def scatter_maps(cell, east, north, weight, acc_ref, cols, first):
    blocks = cols // WIN
    slots = cell.shape[1]
    row = jnp.zeros_like(cell)
    for r in range(1, 8):
        row = row + jnp.where(cell >= r * cols, 1, 0)
    rem = cell - row * cols
    high = (rem // WIN) * 8 + row
    low = rem % WIN
    hit = lax.broadcasted_iota(jnp.int32, (8 * blocks, slots), 0) == high
    terms = []
    for value in (weight, weight * east, weight * north):
        rest = value
        for _ in range(3):
            part = rest.astype(jnp.bfloat16).astype(jnp.float32)
            rest = rest - part
            terms.append(jnp.where(hit, part, 0.0).astype(jnp.bfloat16))
    lhs = jnp.concatenate(terms, axis=0)
    rhs = jnp.where(
        lax.broadcasted_iota(jnp.int32, (WIN, slots), 0) == low, 1.0, 0.0
    ).astype(jnp.bfloat16)
    prod = lax.dot_general(
        lhs, rhs, (((1,), (1,)), ((), ())), preferred_element_type=jnp.float32
    )
    if first:
        acc_ref[...] = prod
    else:
        acc_ref[...] += prod


def split_columns(x):
    source = lax.broadcasted_iota(jnp.int32, (WIN, WIN), 0)
    target = lax.broadcasted_iota(jnp.int32, (WIN, WIN), 1)
    wanted = jnp.where(target < LANES, 2 * target, 2 * target - WIN + 1)
    pick = jnp.where(source == wanted, 1.0, 0.0)
    return jnp.dot(
        x, pick, precision=lax.Precision.HIGHEST, preferred_element_type=jnp.float32
    )


def own_columns(x):
    source = lax.broadcasted_iota(jnp.int32, (WIN, LANES), 0)
    target = lax.broadcasted_iota(jnp.int32, (WIN, LANES), 1)
    column = jnp.where(source < LANES, 2 * source, 2 * source - WIN + 1)
    pick = jnp.where(column == target + HALO, 1.0, 0.0)
    return jnp.dot(
        x, pick, precision=lax.Precision.HIGHEST, preferred_element_type=jnp.float32
    )


def east_of(x):
    even, odd = x[:, :LANES], x[:, LANES:]
    return jnp.concatenate([odd, pltpu.roll(even, LANES - 1, 1)], axis=1)


def west_of(x):
    even, odd = x[:, :LANES], x[:, LANES:]
    return jnp.concatenate([pltpu.roll(odd, 1, 1), even], axis=1)


def up(x):
    return pltpu.roll(x, x.shape[0] - 1, 0)


def down(x):
    return pltpu.roll(x, 1, 0)


def run_sweeps(state, coef, force, count):
    def wide(x):
        return (x, east_of(x), west_of(x))

    def rows(slot, a):
        return (wide(state[slot, 0, a]), wide(state[slot, 1, a]))

    def one(src, dst):
        first = rows(src, 0)
        last_u, last_v = state[src, 0, 7], state[src, 1, 7]
        before = (wide(down(last_u)), wide(down(last_v)))
        here = first
        for a in range(8):
            if a < 7:
                after = rows(src, a + 1)
            else:
                after = (wide(up(state[src, 0, 0])), wide(up(state[src, 1, 0])))
            for f in range(2):
                g = 1 - f
                c = lambda k: coef[f, k, a]
                near = c(0) * here[f][0] + force[f, a]
                near = near + (c(3) * here[f][1] + c(4) * here[f][2])
                over = c(1) * after[f][0] + (c(5) * after[g][1] + c(6) * after[g][2])
                under = c(2) * before[f][0] + (c(7) * before[g][1] + c(8) * before[g][2])
                new = near + (over + under)
                state[dst, f, a] = new
            before, here = here, after

    def two(step, carry):
        one(0, 1)
        one(1, 0)
        return carry

    lax.fori_loop(0, count // 2, two, 0)


def make_coefs(layers, get, state, coef, gain, force):
    strips = state.shape[3]
    index = lax.broadcasted_iota(jnp.int32, (strips, WIN), 0)
    not_top = jnp.where(index == strips - 1, 0.0, 1.0)
    not_low = jnp.where(index == 0, 0.0, 1.0)

    def north(x, a):
        return x[a + 1] if a < 7 else up(x[0]) * not_top

    def south(x, a):
        return x[a - 1] if a > 0 else down(x[7]) * not_low

    u = [get(0, a) for a in range(8)]
    v = [get(1, a) for a in range(8)]
    visc = []
    for a in range(8):
        ux = 0.5 * (north(u, a) - south(u, a))
        vx = 0.5 * (north(v, a) - south(v, a))
        uy = 0.5 * (east_of(u[a]) - west_of(u[a]))
        vy = 0.5 * (east_of(v[a]) - west_of(v[a]))
        shear = uy + vx
        strain = ux * ux + vy * vy + ux * vy + 0.25 * shear * shear + REGULAR
        rate = jnp.exp(jnp.log(strain) * (-1.0 / 3.0))
        visc.append(0.5 * rate * get(6, a) / layers)
        state[0, 0, a] = u[a]
        state[0, 1, a] = v[a]
    for a in range(8):
        here = visc[a]
        vn, vs, ve, vw = north(visc, a), south(visc, a), east_of(here), west_of(here)
        fn, fs, fe, fw = (0.5 * (here + x) for x in (vn, vs, ve, vw))
        drag, inside = get(2, a), get(3, a)
        top = not_top if a == 7 else 1.0
        low = not_low if a == 0 else 1.0
        for f in range(2):
            rg, cg = (4.0, 1.0) if f == 0 else (1.0, 4.0)
            rx, cx = (0.5, 0.25) if f == 0 else (0.25, 0.5)
            spread = rg * (fn + fs) + cg * (fe + fw) + drag
            g = OMEGA * inside / (spread + 1.0 - inside)
            coef[f, 0, a] = inside - g * spread
            coef[f, 1, a] = g * rg * fn * top
            coef[f, 2, a] = g * rg * fs * low
            coef[f, 3, a] = g * cg * fe
            coef[f, 4, a] = g * cg * fw
            coef[f, 5, a] = g * (rx * vn + cx * ve) * top
            coef[f, 6, a] = -g * (rx * vn + cx * vw) * top
            coef[f, 7, a] = -g * (rx * vs + cx * ve) * low
            coef[f, 8, a] = g * (rx * vs + cx * vw) * low
            gain[f, a] = g
            force[f, a] = g * get(4 + f, a)


MESH = pl.DeviceIdType.MESH
RETURN = 16


def exchange(axis, peers, source, target, send_sem, recv_sem):
    copies = []
    for k, peer in enumerate(peers):
        copy = pltpu.make_async_remote_copy(
            src_ref=source(k, peer),
            dst_ref=target(k),
            send_sem=send_sem.at[k],
            recv_sem=recv_sem.at[k],
            device_id={axis: peer},
            device_id_type=MESH,
        )
        copy.start()
        copies.append(copy)
    return copies


def finish(copies):
    for copy in copies:
        copy.wait()


def cut_window(tiles, own, t):
    at = OFF + own * t
    first, skip = at // LANES, at % LANES
    if skip == 0:
        return jnp.concatenate([tiles[first], tiles[first + 1]], axis=1)
    keep = lax.broadcasted_iota(jnp.int32, (8, LANES), 1) < LANES - skip
    turned = [pltpu.roll(tiles[first + j], LANES - skip, 1) for j in range(3)]
    return jnp.concatenate(
        [jnp.where(keep, turned[j], turned[j + 1]) for j in range(2)], axis=1
    )


def join_pieces(pieces, own, q):
    lane = lax.broadcasted_iota(jnp.int32, (8, LANES), 1)
    tile = None
    for s, piece in enumerate(pieces):
        shift = own * s - LANES * q
        if shift + own <= 0 or shift >= LANES:
            continue
        moved = piece if shift % LANES == 0 else pltpu.roll(piece, shift % LANES, 1)
        tile = moved if tile is None else jnp.where(lane >= shift, moved, tile)
    return tile


def fused_kernel(
    strips,
    parts,
    *refs,
):
    args, (vel_ref, grad_ref), held = refs[:12], refs[12:14], refs[14:26]
    (
    obs_out,
    obs_in,
    hard_buf,
    hard_in,
    maps_buf,
    maps_in,
    acc_ref,
    send_a,
    recv_a,
    send_b,
    recv_b,
    send_c,
    recv_c,
    x_ref,
    state,
    coef,
    gain,
    force,
    vel_out,
    vel_in,
    vel_all,
    grad_out,
    grad_in,
    grad_all,
    tile_send,
    tile_recv,
    layer_send,
    layer_recv,
    load_sem,
    ) = refs[26:]
    (
        guess_ref,
        hard_ref,
        thick_ref,
        fric_ref,
        ground_ref,
        mask_ref,
        drive_ref,
        cell_ref,
        east_ref,
        north_ref,
        weight_ref,
        count_ref,
    ) = held
    cols = thick_ref.shape[1]
    group = cols // parts
    own = group // strips
    step = group // LANES
    span = hard_in.shape[1]
    layers = float(hard_ref.shape[0] * parts)
    me, layer = lax.axis_index("tile"), lax.axis_index("layer")
    others = [lax.rem(me + k, strips) for k in range(1, strips)]
    mates = [lax.rem(layer + k, parts) for k in range(1, parts)]

    barrier = pltpu.get_barrier_semaphore()
    for peer in others:
        pl.semaphore_signal(barrier, inc=1, device_id={"tile": peer}, device_id_type=MESH)
    for peer in mates:
        pl.semaphore_signal(barrier, inc=1, device_id={"layer": peer}, device_id_type=MESH)

    arrivals = [
        pltpu.make_async_copy(args[n], held[n], load_sem.at[n]) for n in range(len(args))
    ]
    for n in (7, 8, 9, 10, 11, 1, 2, 0, 3, 4, 5, 6):
        arrivals[n].start()

    for n in (1, 2):
        arrivals[n].wait()
    zero = jnp.zeros((8, LANES), jnp.float32)
    total = hard_buf.shape[0]
    for i in range(total):
        at = (i - 1) * LANES
        if 0 <= at < cols:
            value = hard_ref[0, :, at : at + LANES]
            for k in range(1, hard_ref.shape[0]):
                value = value + hard_ref[k, :, at : at + LANES]
            hard_buf[i] = value * thick_ref[:, at : at + LANES]
        else:
            hard_buf[i] = zero
            for f in range(3):
                maps_buf[f, i] = zero
    for n in (7, 8, 9, 10, 11):
        arrivals[n].wait()
    slot = lax.broadcasted_iota(jnp.int32, (1, cell_ref.shape[3]), 1)
    for d in range(strips):
        obs_out[d, 0:1] = cell_ref[0, 0, d : d + 1].astype(jnp.float32)
        obs_out[d, 1:2] = east_ref[0, 0, d : d + 1]
        obs_out[d, 2:3] = north_ref[0, 0, d : d + 1]
        obs_out[d, 3:4] = jnp.where(slot < count_ref[0, :, d : d + 1], weight_ref[0, 0, d : d + 1], 0.0)

    for n in (0, 3, 4, 5, 6):
        arrivals[n].wait()
    def group_tiles(load):
        tiles = []
        for i in range(span):
            at = group * layer + (i - 1) * LANES
            if 1 <= i <= step:
                tiles.append(load(pl.ds(pl.multiple_of(at, LANES), LANES)))
            else:
                inside = jnp.logical_and(at >= 0, at < cols)
                safe = jnp.where(inside, at, 0)
                value = load(pl.ds(pl.multiple_of(safe, LANES), LANES))
                tiles.append(jnp.where(inside, value, 0.0))
        return tiles

    loads = [
        lambda at: guess_ref[0, :, at],
        lambda at: guess_ref[1, :, at],
        lambda at: fric_ref[:, at] * ground_ref[:, at].astype(jnp.float32),
        lambda at: mask_ref[:, at].astype(jnp.float32),
        lambda at: drive_ref[0, :, at],
        lambda at: drive_ref[1, :, at],
    ]
    for f, load in enumerate(loads):
        tiles = group_tiles(load)
        for t in range(strips):
            send_a[t, f] = cut_window(tiles, own, t)

    def split_all(ref):
        rows = ref[...].reshape(-1, WIN)
        ref[...] = split_columns(rows).reshape(ref.shape)

    split_all(send_a)

    def tile_exchange(n, out, into):
        return exchange(
            "tile",
            others,
            lambda k, peer: out.at[peer],
            lambda k: into.at[me],
            tile_send.at[n],
            tile_recv.at[n],
        )

    pl.semaphore_wait(barrier, strips + parts - 2)
    hard_copies = exchange(
        "layer",
        mates,
        lambda k, peer: hard_buf.at[pl.ds(step * peer, span)],
        lambda k: hard_in.at[k],
        layer_send.at[0],
        layer_recv.at[0],
    )
    obs_copies = tile_exchange(0, obs_out, obs_in)
    a_copies = tile_exchange(1, send_a, recv_a)
    obs_in[me] = obs_out[me]
    recv_a[me] = send_a[me]

    finish(hard_copies)
    tiles = []
    for i in range(span):
        value = hard_buf[step * layer + i]
        for k in range(parts - 1):
            value = value + hard_in[k, i]
        tiles.append(value)
    for t in range(strips):
        send_b[t] = cut_window(tiles, own, t)
    split_all(send_b)
    b_copies = tile_exchange(2, send_b, recv_b)
    recv_b[me] = send_b[me]

    finish(obs_copies)
    for s in range(strips):
        scatter_maps(
            obs_in[s, 0:1].astype(jnp.int32),
            obs_in[s, 1:2],
            obs_in[s, 2:3],
            obs_in[s, 3:4],
            acc_ref,
            cols,
            s == 0,
        )
    n = 8 * (cols // WIN)
    for f in range(3):
        for i in range(cols // LANES):
            at = 3 * f * n + 8 * (i // 2)
            half = slice((i % 2) * LANES, (i % 2 + 1) * LANES)
            maps_buf[f, i + 1] = (
                acc_ref[at : at + 8, half]
                + acc_ref[at + n : at + n + 8, half]
                + acc_ref[at + 2 * n : at + 2 * n + 8, half]
            )
    maps_copies = exchange(
        "layer",
        mates,
        lambda k, peer: maps_buf.at[:, pl.ds(step * peer, span)],
        lambda k: maps_in.at[k],
        layer_send.at[1],
        layer_recv.at[1],
    )

    finish(maps_copies)
    for f in range(3):
        tiles = []
        for i in range(span):
            value = maps_buf[f, step * layer + i]
            for k in range(parts - 1):
                value = value + maps_in[k, f, i]
            tiles.append(value)
        for t in range(strips):
            send_c[t, f] = cut_window(tiles, own, t)
    split_all(send_c)
    c_copies = tile_exchange(3, send_c, recv_c)
    recv_c[me] = send_c[me]

    finish(a_copies)
    finish(b_copies)
    for f in range(6):
        x_ref[f] = jnp.swapaxes(recv_a[:, f], 0, 1)
    x_ref[6] = jnp.swapaxes(recv_b[...], 0, 1)

    def get(f, a):
        return x_ref[f, a]

    make_coefs(layers, get, state, coef, gain, force)
    run_sweeps(state, coef, force, SWEEPS)

    def own_rows(rows):
        picked = own_columns(jnp.concatenate(rows, axis=0))
        return jnp.swapaxes(picked.reshape(8, strips, LANES), 0, 1)

    for f in range(2):
        vel_out[:, f] = own_rows([state[0, f, a] for a in range(8)])
    vel_copies = tile_exchange(4, vel_out, vel_in)
    vel_in[me] = vel_out[me]

    finish(c_copies)
    for f in range(3):
        x_ref[7 + f] = jnp.swapaxes(recv_c[:, f], 0, 1)
    for a in range(8):
        for f in range(2):
            vel = state[0, f, a]
            force[f, a] = gain[f, a] * (vel * get(7, a) - get(8 + f, a))
            gain[f, a] = vel
            state[0, f, a] = jnp.zeros_like(vel)
    run_sweeps(state, coef, force, RETURN)

    def layer_gather(n, every):
        here = every.at[:, pl.ds(step * layer, step)]
        return exchange(
            "layer", mates, lambda k, peer: here, lambda k: here, layer_send.at[n], layer_recv.at[n]
        )

    finish(vel_copies)
    for f in range(2):
        pieces = [vel_in[s, f] for s in range(strips)]
        for q in range(step):
            vel_all[f, step * layer + q] = join_pieces(pieces, own, q)
    gather_copies = layer_gather(2, vel_all)
    run_sweeps(state, coef, force, SWEEPS - RETURN)

    grad_out[...] = own_rows(
        [
            -(get(2, a) * (gain[0, a] * state[0, 0, a] + gain[1, a] * state[0, 1, a]))
            for a in range(8)
        ]
    )
    grad_copies = tile_exchange(5, grad_out, grad_in)
    grad_in[me] = grad_out[me]
    finish(gather_copies)
    for f in range(2):
        for i in range(cols // LANES):
            vel_ref[f, :, i * LANES : (i + 1) * LANES] = vel_all[f, i]
    finish(grad_copies)
    pieces = [grad_in[s] for s in range(strips)]
    for q in range(step):
        grad_all[0, step * layer + q] = join_pieces(pieces, own, q)
    finish(layer_gather(3, grad_all))
    for i in range(cols // LANES):
        grad_ref[:, i * LANES : (i + 1) * LANES] = grad_all[0, i]


def hand_over(vel_ref, grad_ref, vel_out, grad_out, vel_held, grad_held, sems):
    pieces = [
        (vel_ref.at[0], vel_held.at[0], vel_out.at[0]),
        (vel_ref.at[1], vel_held.at[1], vel_out.at[1]),
        (grad_ref, grad_held, grad_out),
    ]
    loads = [
        pltpu.make_async_copy(source, held, sems.at[0, n])
        for n, (source, held, _) in enumerate(pieces)
    ]
    stores = [
        pltpu.make_async_copy(held, target, sems.at[1, n])
        for n, (_, held, target) in enumerate(pieces)
    ]
    for load in loads:
        load.start()
    for load, store in zip(loads, stores):
        load.wait()
        store.start()
    for store in stores:
        store.wait()


def on_device(*fields):
    strips, parts = lax.axis_size("tile"), lax.axis_size("layer")
    cols = fields[2].shape[1]
    slots = fields[7].shape[3]
    group = cols // parts
    own = group // strips
    span = -(-(OFF + own * (strips - 1) + WIN) // LANES)
    total = group // LANES * (parts - 1) + span
    tiles = cols // LANES

    def vmem(*shape):
        return pltpu.VMEM(shape, jnp.float32)

    velocity, gradient = pl.pallas_call(
        functools.partial(fused_kernel, strips, parts),
        out_shape=(
            jax.ShapeDtypeStruct((2, 8, cols), jnp.float32),
            jax.ShapeDtypeStruct((8, cols), jnp.float32),
        ),
        in_specs=[pl.BlockSpec(memory_space=pl.ANY)] * len(fields),
        out_specs=(pl.BlockSpec(memory_space=pltpu.VMEM),) * 2,
        scratch_shapes=[pltpu.VMEM(x.shape, x.dtype) for x in fields]
        + [
            vmem(strips, 4, slots),
            vmem(strips, 4, slots),
            vmem(total, 8, LANES),
            vmem(parts - 1, span, 8, LANES),
            vmem(3, total, 8, LANES),
            vmem(parts - 1, 3, span, 8, LANES),
            vmem(9 * 8 * (cols // WIN), WIN),
            vmem(strips, 6, 8, WIN),
            vmem(strips, 6, 8, WIN),
            vmem(strips, 8, WIN),
            vmem(strips, 8, WIN),
            vmem(strips, 3, 8, WIN),
            vmem(strips, 3, 8, WIN),
            vmem(10, 8, strips, WIN),
            vmem(2, 2, 8, strips, WIN),
            vmem(2, 9, 8, strips, WIN),
            vmem(2, 8, strips, WIN),
            vmem(2, 8, strips, WIN),
            vmem(strips, 2, 8, LANES),
            vmem(strips, 2, 8, LANES),
            vmem(2, tiles, 8, LANES),
            vmem(strips, 8, LANES),
            vmem(strips, 8, LANES),
            vmem(1, tiles, 8, LANES),
            pltpu.SemaphoreType.DMA((6, strips - 1)),
            pltpu.SemaphoreType.DMA((6, strips - 1)),
            pltpu.SemaphoreType.DMA((4, parts - 1)),
            pltpu.SemaphoreType.DMA((4, parts - 1)),
            pltpu.SemaphoreType.DMA((len(fields),)),
        ],
        compiler_params=pltpu.CompilerParams(
            collective_id=0, has_side_effects=True, vmem_limit_bytes=VMEM_LIMIT
        ),
    )(*fields)
    kept = (
        jax.ShapeDtypeStruct(velocity.shape, jnp.float32),
        jax.ShapeDtypeStruct(gradient.shape, jnp.float32),
    )
    return pl.pallas_call(
        hand_over,
        out_shape=kept,
        in_specs=[pl.BlockSpec(memory_space=pl.ANY)] * 2,
        out_specs=(pl.BlockSpec(memory_space=pl.ANY),) * 2,
        scratch_shapes=[
            vmem(*velocity.shape),
            vmem(*gradient.shape),
            pltpu.SemaphoreType.DMA((2, 3)),
        ],
        compiler_params=pltpu.CompilerParams(vmem_limit_bytes=VMEM_LIMIT),
    )(velocity, gradient)


def solution(mesh):
    return jax.shard_map(
        on_device,
        mesh=mesh,
        in_specs=(
            P(None, "tile", None),
            P("layer", "tile", None),
            P("tile", None),
            P("tile", None),
            P("tile", None),
            P("tile", None),
            P(None, "tile", None),
            P("tile", "layer", None, None),
            P("tile", "layer", None, None),
            P("tile", "layer", None, None),
            P("tile", "layer", None, None),
            P("tile", "layer", None),
        ),
        out_specs=(P(None, "tile", None), P("tile", None)),
        check_vma=False,
    )
```
